512 devices in a mesh: tile: 64 (over y_hi, z, core), dir: 8 (over x, y_lo).
Axes of the slice: x: 4, y: 8 (y_hi: 4, y_lo: 2; y = y_hi * 2 + y_lo), z: 8, core: 2. Of those that a mesh axis runs over, the one named last changes fastest.
Arguments:
- coherency: bfloat16 [128, 48, 12, 8, 256], P('tile', 'dir'), may hold values from -0.59765625 to 0.59765625
- observed: bfloat16 [128, 12, 8, 256], P('tile'), may hold values from -12 to 12
- flags: int32 [128, 3], P('tile'), may hold values 0 or 1
- tile_map: int32 [128, 2], P('tile'), may hold values from 0 to 31, as said below
- jones: float32 [48, 8, 512], P('dir', None, 'tile'), may hold values from -6 to 6
Outputs:
- residual: float32 [128, 12, 8, 256], P('tile', None, None, 'dir')
- gradient: float32 [48, 8, 512], P('dir', None, 'tile')
- curvature: float32 [48, 2, 512], P('dir', None, 'tile')
The draws below stay inside these ranges and needn't reach their ends.
Inputs may be any that keep to these rules, and one draw needn't show every extreme that they name: `tile_map`: each row names a station block pair (row block, column block) with row block <= column block; no pair appears twice.
All inputs are finite; a program needn't handle non-finite values. No bound on the sum of `flags` on one device may be relied on, other than what follows from the above.
Results may differ from the reference program's by a relative error of at most 0.00035.
Values sent between devices are 32-bit elements; how exact they have to be, the bound alone decides.
A program may use at most 64 MiB of HBM per device.

```python
import jax
import jax.numpy as jnp
from jax import lax

STATIONS = 512
K = 48
SB = 16
FREQ_CHANNELS = 4
TIMES = 3
SAMPLES = 12
TILES = 128


def draw_tile_map(key, part):
    key = jax.random.fold_in(key, 11)
    blocks = STATIONS // SB
    pairs = blocks * (blocks + 1) // 2
    order = jax.random.permutation(jax.random.fold_in(key, 1), pairs).astype(jnp.int32)
    target = blocks - 1
    found = jnp.argmax(order == target).astype(jnp.int32)
    place = jax.random.randint(jax.random.fold_in(key, 2), (), 0, TILES).astype(jnp.int32)
    selected_entry = order.at[found].set(order[place]).at[place].set(target)[:TILES]
    indices = jnp.arange(blocks, dtype=jnp.int32)
    starts = indices * blocks - indices * (indices - 1) // 2
    row_block = jnp.sum((selected_entry[:, None] >= starts[None, 1:]).astype(jnp.int32), axis=1)
    col_block = row_block + selected_entry - starts[row_block]
    return jnp.stack([row_block, col_block], axis=1).astype(jnp.int32)


def set_ends(drawn, stream_key, low, largest):
    index_at = [jax.random.randint(jax.random.fold_in(stream_key, axis), (), 0, length) for axis, length in enumerate(drawn.shape)]
    widest = drawn.shape.index(max(drawn.shape))
    neighbour = index_at[:widest] + [(index_at[widest] + 1) % drawn.shape[widest]] + index_at[widest + 1:]
    return drawn.at[tuple(index_at)].set(low).at[tuple(neighbour)].set(largest)


def block_levels(own_key, shape, shards, smallest, largest):
    level = 1.0
    for position, blocks in shards:
        draws = jax.random.uniform(jax.random.fold_in(jax.random.fold_in(own_key, 6), position), (blocks,), jnp.float32, smallest / len(shards), largest / len(shards))
        level = level * jnp.repeat(jnp.exp(draws), shape[position] // blocks).reshape((-1,) + (1,) * (len(shape) - 1 - position))
    return level


def normal_values(own_key, extent, spread, limit, split=(), kind=jnp.bfloat16):
    entries = spread * jax.random.normal(own_key, extent, jnp.float32)
    if split:
        entries = entries * block_levels(own_key, extent, split, -0.22, 0.18)
    return jnp.clip(entries, -limit, limit).astype(kind)


def setup_inputs(seed: int = 0) -> dict:
    splits = jax.random.split(jax.random.key(seed), 6)
    coherency = normal_values(splits[0], (TILES, K, SAMPLES, 8, SB * SB), 0.1, 0.59765625, ((0, 64), (1, 8)))
    observed = normal_values(splits[1], (TILES, SAMPLES, 8, SB * SB), 2.0, 12.0, ((0, 64),))
    flags = set_ends((jax.random.randint(splits[2], (TILES, TIMES), 0, 8) < 1).astype(jnp.int32), jax.random.fold_in(splits[2], 1), 0, 1)
    tile_map = draw_tile_map(jax.random.fold_in(splits[5], 71), 0)
    jones = normal_values(splits[4], (K, 8, STATIONS), 1.0, 6.0, ((0, 8), (2, 64)), jnp.float32)
    return {"coherency": coherency, "observed": observed, "flags": flags, "tile_map": tile_map, "jones": jones}


def split_parts(values):
    shape = values.shape[:-2] + (2, 2, values.shape[-1])
    return values[..., 0:4, :].reshape(shape), values[..., 4:8, :].reshape(shape)


def join_parts(re_part, im_part):
    shape = re_part.shape[:-3] + (4, re_part.shape[-1])
    return jnp.concatenate([re_part.reshape(shape), im_part.reshape(shape)], axis=-2)


def complex_product(left_re, left_im, right_re, right_im):
    lre = left_re[..., :, :, None, :]
    lim = left_im[..., :, :, None, :]
    rre = right_re[..., None, :, :, :]
    rim = right_im[..., None, :, :, :]
    return jnp.sum(lre * rre - lim * rim, axis=-3), jnp.sum(lre * rim + lim * rre, axis=-3)


def adjoint(re_part, im_part):
    return jnp.swapaxes(re_part, -3, -2), -jnp.swapaxes(im_part, -3, -2)


def weights(row_flag_mask, block_pair):
    valid_samples = jnp.repeat((1 - row_flag_mask).astype(jnp.float32), FREQ_CHANNELS)
    baseline = jnp.arange(SB * SB, dtype=jnp.int32)
    inner_row = baseline // SB
    inner_col = baseline % SB
    upper_triangle_pairs = jnp.where((block_pair[0] < block_pair[1]) | (inner_row < inner_col), 1.0, 0.0).astype(jnp.float32)
    return valid_samples[:, None, None] * upper_triangle_pairs[None, None, :]


def tile_terms(coher, jones_all, block_pair):
    row_gain_matrix = lax.dynamic_slice_in_dim(jones_all, (block_pair[0] * SB).astype(jnp.int32), SB, 2)
    col_jones = lax.dynamic_slice_in_dim(jones_all, (block_pair[1] * SB).astype(jnp.int32), SB, 2)
    first_antenna = jnp.repeat(row_gain_matrix, SB, axis=2)[:, None]
    station_q = jnp.tile(col_jones, (1, 1, SB))[:, None]
    coh_re, coh_im = split_parts(coher)
    p_re, p_im = split_parts(first_antenna)
    q_re, q_im = split_parts(station_q)
    qh_re, qh_im = adjoint(q_re, q_im)
    m_re, m_im = complex_product(coh_re, coh_im, qh_re, qh_im)
    n_re, n_im = complex_product(p_re, p_im, coh_re, coh_im)
    v_re, v_im = complex_product(p_re, p_im, m_re, m_im)
    predicted = jnp.sum(join_parts(v_re, v_im), axis=0)
    return predicted, (m_re, m_im, n_re, n_im)


def station_terms(residual, weight, products):
    m_re, m_im, n_re, n_im = products
    r_re, r_im = split_parts(residual)
    mh_re, mh_im = adjoint(m_re, m_im)
    g_re, g_im = complex_product(r_re, r_im, mh_re, mh_im)
    row_side = jnp.sum(join_parts(g_re, g_im), axis=1)
    rh_re, rh_im = adjoint(r_re, r_im)
    f_re, f_im = complex_product(rh_re, rh_im, n_re, n_im)
    col_side = jnp.sum(join_parts(f_re, f_im), axis=1)
    row_curv = jnp.sum(jnp.sum(m_re * m_re + m_im * m_im, axis=-2) * weight[None], axis=1)
    column_curvature = jnp.sum(jnp.sum(n_re * n_re + n_im * n_im, axis=-3) * weight[None], axis=1)
    lead = row_side.shape[0]
    grad_row = jnp.sum(row_side.reshape(lead, 8, SB, SB), axis=3)
    grad_col = jnp.sum(col_side.reshape(lead, 8, SB, SB), axis=2)
    curv_row = jnp.sum(row_curv.reshape(lead, 2, SB, SB), axis=3)
    curv_col = jnp.sum(column_curvature.reshape(lead, 2, SB, SB), axis=2)
    return grad_row, grad_col, curv_row, curv_col


def add_block(total, piece, block):
    offset = (block * SB).astype(jnp.int32)
    current = lax.dynamic_slice_in_dim(total, offset, SB, 2)
    return lax.dynamic_update_slice_in_dim(total, current + piece, offset, 2)


def reference(coherency, observed, flags, tile_map, jones):
    def one_tile(carry, inputs):
        grad_total, curv_total = carry
        coher, seen, row_flag_mask, block_pair = inputs
        predicted, products = tile_terms(coher.astype(jnp.float32), jones, block_pair)
        weight = weights(row_flag_mask, block_pair)
        residual = weight * (seen.astype(jnp.float32) - predicted)
        grad_row, grad_col, curv_row, curv_col = station_terms(residual, weight, products)
        grad_total = add_block(add_block(grad_total, grad_row, block_pair[0]), grad_col, block_pair[1])
        curv_total = add_block(add_block(curv_total, curv_row, block_pair[0]), curv_col, block_pair[1])
        return (grad_total, curv_total), residual

    start = (jnp.zeros((K, 8, STATIONS), jnp.float32), jnp.zeros((K, 2, STATIONS), jnp.float32))
    (grad_total, curv_total), residual = lax.scan(one_tile, start, (coherency, observed, flags, tile_map))
    normalizer = 1.0 / (SAMPLES * SB)
    return residual, grad_total * normalizer, curv_total * normalizer
```

```python
import functools

import jax
import jax.numpy as jnp
from jax import lax
from jax.experimental import pallas as pl
from jax.experimental.pallas import tpu as pltpu
from jax.sharding import PartitionSpec as P

MESH = pl.DeviceIdType.MESH
YH, Z, CORES, DIRS = 4, 8, 2, 8
TILES = YH * Z * CORES
SB = 16
F32 = jnp.float32
BF16 = jnp.bfloat16


def hops(offset):
    y, z, c = offset
    return 2 * min(y, YH - y) + min(z, Z - z) + 0.5 * c


FAR_FIRST = sorted(
    (
        (y, z, c)
        for y in range(YH)
        for z in range(Z)
        for c in range(CORES)
        if (y, z, c) != (0, 0, 0)
    ),
    key=lambda o: -hops(o),
)
Z_NEAR_FIRST = (1, 7, 2, 6, 3, 5, 4)
Z_FAR_FIRST = (4, 3, 5, 2, 6, 1, 7)
YC_FAR_FIRST = ((2, 1), (2, 0), (1, 1), (3, 1), (1, 0), (3, 0), (0, 1))


def times_adjoint(a, b):
    re, im = [], []
    for r in range(2):
        for c in range(2):
            x, y = None, None
            for m in range(2):
                ar, ai, br, bi = a[r * 2 + m], a[4 + r * 2 + m], b[c * 2 + m], b[4 + c * 2 + m]
                xr, xi = ar * br + ai * bi, ai * br - ar * bi
                x, y = (xr, xi) if x is None else (x + xr, y + xi)
            re.append(x)
            im.append(y)
    return re + im


def times(a, b):
    re, im = [], []
    for r in range(2):
        for c in range(2):
            x, y = None, None
            for m in range(2):
                ar, ai, br, bi = a[r * 2 + m], a[4 + r * 2 + m], b[m * 2 + c], b[4 + m * 2 + c]
                xr, xi = ar * br - ai * bi, ar * bi + ai * br
                x, y = (xr, xi) if x is None else (x + xr, y + xi)
            re.append(x)
            im.append(y)
    return re + im


def adjoint_times(a, b):
    re, im = [], []
    for r in range(2):
        for c in range(2):
            x, y = None, None
            for m in range(2):
                ar, ai, br, bi = a[m * 2 + r], a[4 + m * 2 + r], b[m * 2 + c], b[4 + m * 2 + c]
                xr, xi = ar * br + ai * bi, ar * bi - ai * br
                x, y = (xr, xi) if x is None else (x + xr, y + xi)
            re.append(x)
            im.append(y)
    return re + im


def fold(values):
    row = lax.broadcasted_iota(jnp.int32, (8, 128), 0)
    low = row < 4
    first = row % 4 < 2
    a, b, c, d = values
    e = jnp.where(low, a, c) + pltpu.roll(jnp.where(low, c, a), 4, 0)
    f = jnp.where(low, b, d) + pltpu.roll(jnp.where(low, d, b), 4, 0)
    return jnp.where(first, e, pltpu.roll(f, 2, 0)) + jnp.where(first, pltpu.roll(e, 6, 0), f)


def split(x):
    high = x.astype(BF16)
    return high, (x - high.astype(F32)).astype(BF16)


def kernel(
    coherency,
    observed,
    flags,
    tile_map,
    jones,
    res_out,
    grad_out,
    curv_out,
    coh_raw,
    obs_raw,
    rows,
    obs_rows,
    coh,
    gains,
    m_all,
    n_all,
    partial,
    taken,
    residual,
    weight,
    val_p,
    val_q,
    pay,
    paid,
    jones_all,
    stage,
    local_sem,
    send_sem,
    recv_sem,
    near_sem,
):
    tile, me = lax.axis_index("tile"), lax.axis_index("dir")
    y, z, core = tile // (Z * CORES), tile // CORES % Z, tile % CORES

    def at(dy, dz, dc):
        return (
            lax.rem(y + dy, YH) * (Z * CORES)
            + lax.rem(z + dz, Z) * CORES
            + lax.rem(core + dc, CORES)
        )

    def remote(src, dst, send, recv, device):
        return pltpu.make_async_remote_copy(
            src_ref=src,
            dst_ref=dst,
            send_sem=send,
            recv_sem=recv,
            device_id=device,
            device_id_type=MESH,
        )

    get_coh = pltpu.make_async_copy(coherency, coh_raw, local_sem.at[0])
    get_obs = pltpu.make_async_copy(observed, obs_raw, local_sem.at[1])
    get_coh.start()
    get_obs.start()

    barrier = pltpu.get_barrier_semaphore()
    greeted = (
        [(at(0, dz, 0), me) for dz in Z_FAR_FIRST]
        + [(at(dy, 0, dc), me) for dy, dc in YC_FAR_FIRST]
        + [(tile, lax.rem(me + r, DIRS)) for r in range(1, DIRS)]
    )
    for device in greeted:
        pl.semaphore_signal(barrier, inc=1, device_id=device, device_id_type=MESH)

    packed = jnp.zeros((8, 128), F32)
    for k in range(6):
        wide = jnp.concatenate([jones[k], jnp.zeros((8, 120), F32)], axis=1)
        packed = packed + (pltpu.roll(wide, 8 * k, 1) if k else wide)
    packed = packed[0:4] + pltpu.roll(packed, 64, 1)[4:8]
    jones_all[tile] = packed

    get_coh.wait()
    get_obs.wait()

    def to_rows(k, carry):
        for t in range(2):
            for s in range(12):
                block = coh_raw[t, k, s].astype(F32)
                for h in range(2):
                    rows[h, k, pl.ds((s * 2 + t) * 8, 8), :] = block[:, h * 128 : h * 128 + 128]
        for h in range(2):
            for c in range(8):
                coh[k, h, c] = rows[h, k, pl.ds(c, 24, stride=8), :].reshape(3, 8, 128)
        return carry

    lax.fori_loop(0, 6, to_rows, 0)
    for t in range(2):
        for s in range(12):
            block = obs_raw[t, s].astype(F32)
            for h in range(2):
                obs_rows[h, pl.ds((s * 2 + t) * 8, 8), :] = block[:, h * 128 : h * 128 + 128]

    odd_row = lax.broadcasted_iota(jnp.int32, (8, 128), 0) % 2 == 1
    for h in range(2):
        baseline = lax.broadcasted_iota(jnp.int32, (8, 128), 1) + 128 * h
        upper = jnp.where(baseline // SB < baseline % SB, 1, 0)
        for g in range(3):
            both = []
            for t in range(2):
                ahead = jnp.where(tile_map[t, 0] < tile_map[t, 1], 1, 0)
                kept = 1 - flags[t, g]
                both.append((jnp.maximum(upper, ahead) * kept).astype(F32))
            weight[h, g] = jnp.where(odd_row, both[1], both[0])

    pl.semaphore_wait(barrier, len(greeted))

    mine = jones_all.at[tile]
    for dz in Z_FAR_FIRST:
        remote(mine, mine, send_sem.at[0], near_sem.at[dz], (at(0, dz, 0), me)).start()
    for dy, dc in YC_FAR_FIRST:
        remote(mine, mine, send_sem.at[0], recv_sem.at[0], (at(dy, 0, dc), me)).start()
    for dz in Z_NEAR_FIRST:
        piece = jones_all.at[at(0, Z - dz, 0)]
        remote(piece, piece, send_sem.at[0], near_sem.at[dz], (at(0, dz, 0), me)).wait_recv()
        for dy, dc in YC_FAR_FIRST:
            remote(piece, piece, send_sem.at[0], recv_sem.at[0], (at(dy, 0, dc), me)).start()
    count = 7 * Z
    far = jones_all.at[pl.ds(0, count)]
    remote(far, far, send_sem.at[0], recv_sem.at[0], (at(1, 0, 0), me)).wait_recv()

    row = lax.broadcasted_iota(jnp.int32, (6, 8, 256), 1)
    direction = lax.broadcasted_iota(jnp.int32, (6, 8, 256), 0)
    lane = lax.broadcasted_iota(jnp.int32, (6, 8, 256), 2)
    own = lane % 128 // 8 == row // 4 * 8 + direction
    station = lax.broadcasted_iota(jnp.int32, (256, 256), 0)
    station = station // 128 * 8 + station % 8
    baseline = lax.broadcasted_iota(jnp.int32, (256, 256), 1)
    for side in range(2):
        spread = jnp.where(station == (baseline % SB if side else baseline // SB), 1.0, 0.0)
        spread = spread.astype(BF16)
        for t in range(2):
            block = tile_map[t, side]
            both = jnp.concatenate([jones_all[2 * block], jones_all[2 * block + 1]], axis=1)
            both = jnp.concatenate([both, both], axis=0)
            chosen = jnp.where(own, both[None], 0.0).reshape(48, 256)
            high, low = split(chosen)
            full = jnp.dot(high, spread, preferred_element_type=F32)
            full = full + jnp.dot(low, spread, preferred_element_type=F32)
            for h in range(2):
                gains[side, t, h] = full[:, h * 128 : h * 128 + 128].reshape(6, 8, 128)

    def gain(side, k, h):
        return [
            jnp.where(
                odd_row,
                jnp.broadcast_to(gains[side, 1, h, k, pl.ds(c, 1), :], (8, 128)),
                jnp.broadcast_to(gains[side, 0, h, k, pl.ds(c, 1), :], (8, 128)),
            )
            for c in range(8)
        ]

    for h in range(2):

        def add_direction(k, total, h=h):
            p, q = gain(0, k, h), gain(1, k, h)
            out = []
            for g in range(3):
                m = times_adjoint([coh[k, h, c, g] for c in range(8)], q)
                for c in range(8):
                    m_all[k, h, c, g] = m[c]
                v = times(p, m)
                out += [total[g * 8 + c] + v[c] for c in range(8)]
            return tuple(out)

        total = lax.fori_loop(0, 6, add_direction, (jnp.zeros((8, 128), F32),) * 24)
        for g in range(3):
            for c in range(8):
                partial[c, h, g] = total[g * 8 + c]

    for r in range(1, DIRS):
        other = lax.rem(me + r, DIRS)
        remote(
            partial.at[other], taken.at[r - 1], send_sem.at[1], recv_sem.at[1], (tile, other)
        ).start()

    val_p[...] = jnp.zeros_like(val_p)
    val_q[...] = jnp.zeros_like(val_q)
    for h in range(2):

        def two_directions(pair, carry, h=h):
            rows_p, rows_q = [], []
            for j in range(2):
                k = pair * 2 + j
                p = gain(0, k, h)
                cp, cq = [0.0, 0.0], [0.0, 0.0]
                for g in range(3):
                    n = times(p, [coh[k, h, c, g] for c in range(8)])
                    for c in range(8):
                        n_all[k, h, c, g] = n[c]
                    m = [m_all[k, h, c, g] for c in range(8)]
                    w = weight[h, g]
                    for c in range(2):
                        cp[c] = cp[c] + w * sum(m[e] * m[e] for e in (2 * c, 2 * c + 1, 4 + 2 * c, 5 + 2 * c))
                        cq[c] = cq[c] + w * sum(n[e] * n[e] for e in (c, c + 2, c + 4, c + 6))
                rows_p += cp
                rows_q += cq
            val_p[12 + pair, :, h * 128 : h * 128 + 128] = fold(rows_p)
            val_q[12 + pair, :, h * 128 : h * 128 + 128] = fold(rows_q)
            return carry

        lax.fori_loop(0, 3, two_directions, 0)

    remote(taken, taken, send_sem.at[1], recv_sem.at[1], (tile, me)).wait_recv()
    for h in range(2):
        model = partial[me, h]
        for r in range(DIRS - 1):
            model = model + taken[r, h]
        seen = obs_rows[h, pl.ds(me, 24, stride=8), :].reshape(3, 8, 128)
        residual[me, h] = weight[h] * (seen - model)

    for r in range(1, DIRS):
        other = lax.rem(me + r, DIRS)
        remote(
            residual.at[me], residual.at[me], send_sem.at[2], recv_sem.at[2], (tile, other)
        ).start()
    seven = residual.at[pl.ds(0, DIRS - 1)]
    remote(seven, seven, send_sem.at[2], recv_sem.at[2], (tile, me)).wait_recv()

    for h in range(2):

        def one_direction(k, carry, h=h):
            a, b = None, None
            for g in range(3):
                res = [residual[c, h, g] for c in range(8)]
                u = times_adjoint(res, [m_all[k, h, c, g] for c in range(8)])
                v = adjoint_times(res, [n_all[k, h, c, g] for c in range(8)])
                a = u if a is None else [i + j for i, j in zip(a, u)]
                b = v if b is None else [i + j for i, j in zip(b, v)]
            for j in range(2):
                val_p[2 * k + j, :, h * 128 : h * 128 + 128] = fold(a[4 * j : 4 * j + 4])
                val_q[2 * k + j, :, h * 128 : h * 128 + 128] = fold(b[4 * j : 4 * j + 4])
            return carry

        lax.fori_loop(0, 6, one_direction, 0)

    place = lax.broadcasted_iota(jnp.int32, (16, 256), 0)
    place = place // 8 * 4 + place // 4 % 2 * 8 + place % 4
    baseline = lax.broadcasted_iota(jnp.int32, (16, 256), 1)
    even = lax.broadcasted_iota(jnp.int32, (8, 128), 1) % 2 == 0
    parts = []
    for side, val in ((0, val_p), (1, val_q)):
        gather = jnp.where(place == (baseline % SB if side else baseline // SB), 1.0, 0.0)
        gather = gather.astype(BF16)
        high, low = split(val[...].reshape(128, 256))
        dims = (((1,), (1,)), ((), ()))
        sums = lax.dot_general(gather, high, dims, preferred_element_type=F32)
        sums = sums + lax.dot_general(gather, low, dims, preferred_element_type=F32)
        top, bottom = sums[0:8], sums[8:16]
        parts.append(
            (
                side,
                0,
                jnp.where(even, top, 0.0) + pltpu.roll(jnp.where(even, bottom, 0.0), 1, 1),
            )
        )
        parts.append(
            (
                side,
                1,
                pltpu.roll(jnp.where(even, 0.0, top), 127, 1) + jnp.where(even, 0.0, bottom),
            )
        )

    for b in range(TILES // 2):
        block = jnp.zeros((8, 128), F32)
        for side, t, part in parts:
            block = block + jnp.where(tile_map[t, side] == b, part, 0.0)
        pay[2 * b] = block[0:4]
        pay[2 * b + 1] = block[4:8]

    for number, (dy, dz, dc) in enumerate(FAR_FIRST):
        owner = at(dy, dz, dc)
        remote(
            pay.at[owner], paid.at[number], send_sem.at[3], recv_sem.at[3], (owner, me)
        ).start()

    half, part = me // 4, me % 4
    for c in range(8):
        wide = residual[c, half].reshape(24, 128)
        wide = pltpu.roll(wide, lax.rem(128 - 32 * part, 128), 1)
        stage[pl.ds(c, 24, stride=8), :] = wide
    for t in range(2):
        for s in range(12):
            res_out[t, s] = stage[pl.ds((s * 2 + t) * 8, 8), 0:32]

    remote(paid, paid, send_sem.at[3], recv_sem.at[3], (tile, me)).wait_recv()
    total = pay[tile] + jnp.sum(paid[...], axis=0)
    wide = jnp.concatenate([total, pltpu.roll(total, 127, 1)], axis=0) * (1.0 / (12 * SB))
    pick = jnp.where(
        lax.broadcasted_iota(jnp.int32, (64, 128), 1)
        == 2 * lax.broadcasted_iota(jnp.int32, (64, 128), 0),
        1.0,
        0.0,
    ).astype(BF16)
    high, low = split(wide)
    rest = (wide - high.astype(F32) - low.astype(F32)).astype(BF16)
    dims = (((1,), (1,)), ((), ()))
    owned = sum(
        lax.dot_general(pick, x, dims, preferred_element_type=F32) for x in (high, low, rest)
    )
    grad_out[...] = owned[0:48].reshape(6, 8, 8)
    for k in range(6):
        curv_out[k] = owned[48 + 2 * k : 50 + 2 * k]

    sent = jones_all.at[pl.ds(0, TILES - 1)]
    remote(sent, sent, send_sem.at[0], recv_sem.at[0], (tile, me)).wait_send()
    remote(taken, taken, send_sem.at[1], recv_sem.at[1], (tile, me)).wait_send()
    remote(seven, seven, send_sem.at[2], recv_sem.at[2], (tile, me)).wait_send()
    remote(paid, paid, send_sem.at[3], recv_sem.at[3], (tile, me)).wait_send()


def body(coherency, observed, flags, tile_map, jones):
    vmem, smem, anywhere = (
        pl.BlockSpec(memory_space=m) for m in (pltpu.VMEM, pltpu.SMEM, pl.ANY)
    )
    scratch = [
        pltpu.VMEM((2, 6, 12, 8, 256), BF16),
        pltpu.VMEM((2, 12, 8, 256), BF16),
        pltpu.VMEM((2, 6, 192, 128), F32),
        pltpu.VMEM((2, 192, 128), F32),
        pltpu.VMEM((6, 2, 8, 3, 8, 128), F32),
        pltpu.VMEM((2, 2, 2, 6, 8, 128), F32),
        pltpu.VMEM((6, 2, 8, 3, 8, 128), F32),
        pltpu.VMEM((6, 2, 8, 3, 8, 128), F32),
        pltpu.VMEM((8, 2, 3, 8, 128), F32),
        pltpu.VMEM((7, 2, 3, 8, 128), F32),
        pltpu.VMEM((8, 2, 3, 8, 128), F32),
        pltpu.VMEM((2, 3, 8, 128), F32),
        pltpu.VMEM((16, 8, 256), F32),
        pltpu.VMEM((16, 8, 256), F32),
        pltpu.VMEM((TILES, 4, 128), F32),
        pltpu.VMEM((TILES - 1, 4, 128), F32),
        pltpu.VMEM((TILES, 4, 128), F32),
        pltpu.VMEM((192, 128), F32),
        pltpu.SemaphoreType.DMA((2,)),
        pltpu.SemaphoreType.DMA((4,)),
        pltpu.SemaphoreType.DMA((4,)),
        pltpu.SemaphoreType.DMA((Z,)),
    ]
    return pl.pallas_call(
        kernel,
        out_shape=(
            jax.ShapeDtypeStruct((2, 12, 8, 32), F32),
            jax.ShapeDtypeStruct((6, 8, 8), F32),
            jax.ShapeDtypeStruct((6, 2, 8), F32),
        ),
        in_specs=[anywhere, anywhere, smem, smem, vmem],
        out_specs=(vmem, vmem, vmem),
        scratch_shapes=scratch,
        compiler_params=pltpu.CompilerParams(
            collective_id=0, has_side_effects=True, vmem_limit_bytes=40 * 1024 * 1024
        ),
    )(coherency, observed, flags, tile_map, jones)


def solution(mesh):
    return jax.shard_map(
        body,
        mesh=mesh,
        in_specs=(
            P("tile", "dir", None, None, None),
            P("tile", None, None, None),
            P("tile", None),
            P("tile", None),
            P("dir", None, "tile"),
        ),
        out_specs=(P("tile", None, None, "dir"), P("dir", None, "tile"), P("dir", None, "tile")),
        check_vma=False,
    )
```

```python
import functools

import jax
import jax.numpy as jnp
from jax import lax
from jax.experimental import pallas as pl
from jax.experimental.pallas import tpu as pltpu
from jax.sharding import PartitionSpec as P

MESH = pl.DeviceIdType.MESH
YH, Z, CORES, DIRS = 4, 8, 2, 8
TILES = YH * Z * CORES
SB = 16
F32 = jnp.float32
BF16 = jnp.bfloat16


def hops(offset):
    y, z, c = offset
    return 2 * min(y, YH - y) + min(z, Z - z) + 0.5 * c


FAR_FIRST = sorted(
    (
        (y, z, c)
        for y in range(YH)
        for z in range(Z)
        for c in range(CORES)
        if (y, z, c) != (0, 0, 0)
    ),
    key=lambda o: -hops(o),
)
Z_NEAR_FIRST = (1, 7, 2, 6, 3, 5, 4)
Z_FAR_FIRST = (4, 3, 5, 2, 6, 1, 7)
YC_FAR_FIRST = ((2, 1), (2, 0), (1, 1), (3, 1), (1, 0), (3, 0), (0, 1))


def times_adjoint(a, b):
    re, im = [], []
    for r in range(2):
        for c in range(2):
            x, y = None, None
            for m in range(2):
                ar, ai, br, bi = a[r * 2 + m], a[4 + r * 2 + m], b[c * 2 + m], b[4 + c * 2 + m]
                xr, xi = ar * br + ai * bi, ai * br - ar * bi
                x, y = (xr, xi) if x is None else (x + xr, y + xi)
            re.append(x)
            im.append(y)
    return re + im


def times(a, b):
    re, im = [], []
    for r in range(2):
        for c in range(2):
            x, y = None, None
            for m in range(2):
                ar, ai, br, bi = a[r * 2 + m], a[4 + r * 2 + m], b[m * 2 + c], b[4 + m * 2 + c]
                xr, xi = ar * br - ai * bi, ar * bi + ai * br
                x, y = (xr, xi) if x is None else (x + xr, y + xi)
            re.append(x)
            im.append(y)
    return re + im


def adjoint_times(a, b):
    re, im = [], []
    for r in range(2):
        for c in range(2):
            x, y = None, None
            for m in range(2):
                ar, ai, br, bi = a[m * 2 + r], a[4 + m * 2 + r], b[m * 2 + c], b[4 + m * 2 + c]
                xr, xi = ar * br + ai * bi, ar * bi - ai * br
                x, y = (xr, xi) if x is None else (x + xr, y + xi)
            re.append(x)
            im.append(y)
    return re + im


def fold(values):
    row = lax.broadcasted_iota(jnp.int32, (8, 128), 0)
    first, even = row % 4 < 2, row % 2 == 0
    a, b, c, d = values
    e = jnp.where(first, a, pltpu.roll(c, 2, 0)) + jnp.where(first, pltpu.roll(a, 6, 0), c)
    f = jnp.where(first, b, pltpu.roll(d, 2, 0)) + jnp.where(first, pltpu.roll(b, 6, 0), d)
    return jnp.where(even, e, pltpu.roll(f, 1, 0)) + jnp.where(even, pltpu.roll(e, 7, 0), f)


def row_of(t, s):
    return s // 4 * 8 + t * 4 + s % 4


def split(x):
    high = x.astype(BF16)
    return high, (x - high.astype(F32)).astype(BF16)


def kernel(
    coherency,
    observed,
    flags_in,
    tile_map_in,
    jones_in,
    res_out,
    grad_out,
    curv_out,
    coh_raw,
    obs_raw,
    rows,
    obs_rows,
    coh,
    gains,
    m_all,
    n_all,
    partial,
    taken,
    residual,
    weight,
    val_p,
    val_q,
    pay,
    paid,
    jones_all,
    stage,
    collect,
    flags,
    tile_map,
    jones,
    local_sem,
    send_sem,
    recv_sem,
    near_sem,
):
    tile, me = lax.axis_index("tile"), lax.axis_index("dir")
    y, z, core = tile // (Z * CORES), tile // CORES % Z, tile % CORES

    def at(dy, dz, dc):
        return (
            lax.rem(y + dy, YH) * (Z * CORES)
            + lax.rem(z + dz, Z) * CORES
            + lax.rem(core + dc, CORES)
        )

    def remote(src, dst, send, recv, device):
        return pltpu.make_async_remote_copy(
            src_ref=src,
            dst_ref=dst,
            send_sem=send,
            recv_sem=recv,
            device_id=device,
            device_id_type=MESH,
        )

    barrier = pltpu.get_barrier_semaphore()
    greeted = (
        [(at(0, dz, 0), me) for dz in Z_FAR_FIRST]
        + [(at(dy, 0, dc), me) for dy, dc in YC_FAR_FIRST]
        + [(tile, lax.rem(me + r, DIRS)) for r in range(1, DIRS)]
    )
    for device in greeted:
        pl.semaphore_signal(barrier, inc=1, device_id=device, device_id_type=MESH)

    here = [
        pltpu.make_async_copy(src, dst, local_sem.at[number])
        for number, (src, dst) in enumerate(
            (
                (jones_in, jones),
                (flags_in, flags),
                (tile_map_in, tile_map),
                (coherency, coh_raw),
                (observed, obs_raw),
            )
        )
    ]
    for copy in here:
        copy.start()

    here[0].wait()
    packed = jnp.zeros((8, 128), F32)
    for k in range(6):
        wide = jnp.concatenate([jones[k], jnp.zeros((8, 120), F32)], axis=1)
        packed = packed + (pltpu.roll(wide, 8 * k, 1) if k else wide)
    packed = packed[0:4] + pltpu.roll(packed, 64, 1)[4:8]
    jones_all[tile] = packed

    pl.semaphore_wait(barrier, len(greeted))

    mine = jones_all.at[tile]
    for dz in Z_FAR_FIRST:
        remote(mine, mine, send_sem.at[0], near_sem.at[dz], (at(0, dz, 0), me)).start()
    for dy, dc in YC_FAR_FIRST:
        remote(mine, mine, send_sem.at[0], recv_sem.at[0], (at(dy, 0, dc), me)).start()
    for copy in here[1:]:
        copy.wait()

    def to_rows(k, carry):
        for t in range(2):
            for s in range(12):
                block = coh_raw[t, k, s].astype(F32)
                for h in range(2):
                    rows[h, k, pl.ds(row_of(t, s) * 8, 8), :] = block[:, h * 128 : h * 128 + 128]
        for h in range(2):
            for c in range(8):
                coh[k, h, c] = rows[h, k, pl.ds(c, 24, stride=8), :].reshape(3, 8, 128)
        return carry

    lax.fori_loop(0, 6, to_rows, 0)
    for t in range(2):
        for s in range(12):
            block = obs_raw[t, s].astype(F32)
            for h in range(2):
                obs_rows[h, pl.ds(row_of(t, s) * 8, 8), :] = block[:, h * 128 : h * 128 + 128]

    second = lax.broadcasted_iota(jnp.int32, (8, 128), 0) >= 4
    for h in range(2):
        baseline = lax.broadcasted_iota(jnp.int32, (8, 128), 1) + 128 * h
        upper = jnp.where(baseline // SB < baseline % SB, 1, 0)
        for g in range(3):
            both = []
            for t in range(2):
                ahead = jnp.where(tile_map[t, 0] < tile_map[t, 1], 1, 0)
                kept = 1 - flags[t, g]
                both.append((jnp.maximum(upper, ahead) * kept).astype(F32))
            weight[h, g] = jnp.where(second, both[1], both[0])

    baseline = lax.broadcasted_iota(jnp.int32, (256, 256), 0)
    station = lax.broadcasted_iota(jnp.int32, (256, 256), 1)
    station = station // 128 * 8 + station % 8
    for side in range(2):
        own = station == (baseline % SB if side else baseline // SB)
        collect[side] = jnp.where(own, 1.0, 0.0).astype(BF16)
    val_p[15] = jnp.zeros((8, 256), F32)
    val_q[15] = jnp.zeros((8, 256), F32)

    for dz in Z_NEAR_FIRST:
        piece = jones_all.at[at(0, Z - dz, 0)]
        remote(piece, piece, send_sem.at[0], near_sem.at[dz], (at(0, dz, 0), me)).wait_recv()
        for dy, dc in YC_FAR_FIRST:
            remote(piece, piece, send_sem.at[0], recv_sem.at[0], (at(dy, 0, dc), me)).start()
    count = 7 * Z
    far = jones_all.at[pl.ds(0, count)]
    remote(far, far, send_sem.at[0], recv_sem.at[0], (at(1, 0, 0), me)).wait_recv()

    row = lax.broadcasted_iota(jnp.int32, (6, 8, 256), 1)
    direction = lax.broadcasted_iota(jnp.int32, (6, 8, 256), 0)
    lane = lax.broadcasted_iota(jnp.int32, (6, 8, 256), 2)
    own = lane % 128 // 8 == row // 4 * 8 + direction
    station = lax.broadcasted_iota(jnp.int32, (256, 256), 0)
    station = station // 128 * 8 + station % 8
    baseline = lax.broadcasted_iota(jnp.int32, (256, 256), 1)
    for side in range(2):
        spread = jnp.where(station == (baseline % SB if side else baseline // SB), 1.0, 0.0)
        spread = spread.astype(BF16)
        for t in range(2):
            block = tile_map[t, side]
            both = jnp.concatenate([jones_all[2 * block], jones_all[2 * block + 1]], axis=1)
            both = jnp.concatenate([both, both], axis=0)
            chosen = jnp.where(own, both[None], 0.0).reshape(48, 256)
            high, low = split(chosen)
            full = jnp.dot(high, spread, preferred_element_type=F32)
            full = full + jnp.dot(low, spread, preferred_element_type=F32)
            for h in range(2):
                gains[side, t, h] = full[:, h * 128 : h * 128 + 128].reshape(6, 8, 128)

    def gain(side, k, h):
        return [
            jnp.where(
                second,
                jnp.broadcast_to(gains[side, 1, h, k, pl.ds(c, 1), :], (8, 128)),
                jnp.broadcast_to(gains[side, 0, h, k, pl.ds(c, 1), :], (8, 128)),
            )
            for c in range(8)
        ]

    for h in range(2):

        def add_direction(k, total, h=h):
            p, q = gain(0, k, h), gain(1, k, h)
            out = []
            for g in range(3):
                m = times_adjoint([coh[k, h, c, g] for c in range(8)], q)
                for c in range(8):
                    m_all[k, h, c, g] = m[c]
                v = times(p, m)
                out += [total[g * 8 + c] + v[c] for c in range(8)]
            return tuple(out)

        total = lax.fori_loop(0, 6, add_direction, (jnp.zeros((8, 128), F32),) * 24)
        for g in range(3):
            for c in range(8):
                partial[c, h, g] = total[g * 8 + c]

        for r in range(1, DIRS):
            other = lax.rem(me + r, DIRS)
            remote(
                partial.at[other, h],
                taken.at[h, r - 1],
                send_sem.at[1],
                recv_sem.at[1 + h],
                (tile, other),
            ).start()

    for h in range(2):

        def two_directions(pair, carry, h=h):
            rows_p, rows_q = [], []
            for j in range(2):
                k = pair * 2 + j
                p = gain(0, k, h)
                cp, cq = [0.0, 0.0], [0.0, 0.0]
                for g in range(3):
                    n = times(p, [coh[k, h, c, g] for c in range(8)])
                    for c in range(8):
                        n_all[k, h, c, g] = n[c]
                    m = [m_all[k, h, c, g] for c in range(8)]
                    w = weight[h, g]
                    for c in range(2):
                        cp[c] = cp[c] + w * sum(m[e] * m[e] for e in (2 * c, 2 * c + 1, 4 + 2 * c, 5 + 2 * c))
                        cq[c] = cq[c] + w * sum(n[e] * n[e] for e in (c, c + 2, c + 4, c + 6))
                rows_p += cp
                rows_q += cq
            val_p[12 + pair, :, h * 128 : h * 128 + 128] = fold(rows_p)
            val_q[12 + pair, :, h * 128 : h * 128 + 128] = fold(rows_q)
            return carry

        lax.fori_loop(0, 3, two_directions, 0)

    for h in range(2):
        got = taken.at[h]
        remote(got, got, send_sem.at[1], recv_sem.at[1 + h], (tile, me)).wait_recv()
        model = partial[me, h]
        for r in range(DIRS - 1):
            model = model + taken[h, r]
        seen = obs_rows[h, pl.ds(me, 24, stride=8), :].reshape(3, 8, 128)
        residual[h, me] = weight[h] * (seen - model)
        done = residual.at[h, me]
        for r in range(1, DIRS):
            other = lax.rem(me + r, DIRS)
            remote(done, done, send_sem.at[2], recv_sem.at[3 + h], (tile, other)).start()

    for h in range(2):
        got = residual.at[h, pl.ds(0, DIRS - 1)]
        remote(got, got, send_sem.at[2], recv_sem.at[3 + h], (tile, me)).wait_recv()

        def one_direction(k, carry, h=h):
            a, b = None, None
            for g in range(3):
                res = [residual[h, c, g] for c in range(8)]
                u = times_adjoint(res, [m_all[k, h, c, g] for c in range(8)])
                v = adjoint_times(res, [n_all[k, h, c, g] for c in range(8)])
                a = u if a is None else [i + j for i, j in zip(a, u)]
                b = v if b is None else [i + j for i, j in zip(b, v)]
            for j in range(2):
                val_p[2 * k + j, :, h * 128 : h * 128 + 128] = fold(a[4 * j : 4 * j + 4])
                val_q[2 * k + j, :, h * 128 : h * 128 + 128] = fold(b[4 * j : 4 * j + 4])
            return carry

        lax.fori_loop(0, 6, one_direction, 0)

    group = lax.broadcasted_iota(jnp.int32, (8, 128), 1) // 8
    parts = []
    for side, val in ((0, val_p), (1, val_q)):
        high, low = split(val[...].reshape(128, 256))
        sums = jnp.dot(high, collect[side], preferred_element_type=F32)
        sums = sums + jnp.dot(low, collect[side], preferred_element_type=F32)
        sums = sums.reshape(16, 8, 256)
        halves = []
        for h in range(2):
            piece = jnp.zeros((8, 128), F32)
            for g in range(15):
                piece = jnp.where(group == g, sums[g, :, h * 128 : h * 128 + 128], piece)
            halves.append(piece)
        parts.append((side, 0, jnp.where(second, pltpu.roll(halves[1], 4, 0), halves[0])))
        parts.append((side, 1, jnp.where(second, halves[1], pltpu.roll(halves[0], 4, 0))))

    for b in range(TILES // 2):
        block = jnp.zeros((8, 128), F32)
        for side, t, part in parts:
            block = block + jnp.where(tile_map[t, side] == b, part, 0.0)
        pay[2 * b] = block[0:4]
        pay[2 * b + 1] = block[4:8]

    for number, (dy, dz, dc) in enumerate(FAR_FIRST):
        owner = at(dy, dz, dc)
        remote(
            pay.at[owner], paid.at[number], send_sem.at[3], recv_sem.at[5], (owner, me)
        ).start()

    half, part = me // 4, me % 4
    for c in range(8):
        wide = residual[half, c].reshape(24, 128)
        wide = pltpu.roll(wide, lax.rem(128 - 32 * part, 128), 1)
        stage[pl.ds(c, 24, stride=8), :] = wide
    for t in range(2):
        for s in range(12):
            res_out[t, s] = stage[pl.ds(row_of(t, s) * 8, 8), 0:32]

    remote(paid, paid, send_sem.at[3], recv_sem.at[5], (tile, me)).wait_recv()
    terms = [pay[tile]] + [paid[number] for number in range(TILES - 1)]
    while len(terms) > 1:
        terms = [a + b for a, b in zip(terms[::2], terms[1::2])]
    total = terms[0] * (1.0 / (12 * SB))
    moved = [(pltpu.roll(total, 128 - 8 * g, 1) if g else total)[:, 0:8] for g in range(15)]
    for k in range(6):
        grad_out[k] = jnp.concatenate(moved[2 * k : 2 * k + 2], axis=0)
        curv_out[k] = moved[12 + k // 2][k % 2 * 2 : k % 2 * 2 + 2]

    sent = jones_all.at[pl.ds(0, TILES - 1)]
    remote(sent, sent, send_sem.at[0], recv_sem.at[0], (tile, me)).wait_send()
    remote(taken, taken, send_sem.at[1], recv_sem.at[1], (tile, me)).wait_send()
    remote(taken, taken, send_sem.at[2], recv_sem.at[1], (tile, me)).wait_send()
    remote(paid, paid, send_sem.at[3], recv_sem.at[5], (tile, me)).wait_send()


def body(coherency, observed, flags, tile_map, jones):
    vmem, hbm = (pl.BlockSpec(memory_space=m) for m in (pltpu.VMEM, pltpu.HBM))
    scratch = [
        pltpu.VMEM((2, 6, 12, 8, 256), BF16),
        pltpu.VMEM((2, 12, 8, 256), BF16),
        pltpu.VMEM((2, 6, 192, 128), F32),
        pltpu.VMEM((2, 192, 128), F32),
        pltpu.VMEM((6, 2, 8, 3, 8, 128), F32),
        pltpu.VMEM((2, 2, 2, 6, 8, 128), F32),
        pltpu.VMEM((6, 2, 8, 3, 8, 128), F32),
        pltpu.VMEM((6, 2, 8, 3, 8, 128), F32),
        pltpu.VMEM((8, 2, 3, 8, 128), F32),
        pltpu.VMEM((2, 7, 3, 8, 128), F32),
        pltpu.VMEM((2, 8, 3, 8, 128), F32),
        pltpu.VMEM((2, 3, 8, 128), F32),
        pltpu.VMEM((16, 8, 256), F32),
        pltpu.VMEM((16, 8, 256), F32),
        pltpu.VMEM((TILES, 4, 128), F32),
        pltpu.VMEM((TILES - 1, 4, 128), F32),
        pltpu.VMEM((TILES, 4, 128), F32),
        pltpu.VMEM((192, 128), F32),
        pltpu.VMEM((2, 256, 256), BF16),
        pltpu.SMEM((2, 3), jnp.int32),
        pltpu.SMEM((2, 2), jnp.int32),
        pltpu.VMEM((6, 8, 8), F32),
        pltpu.SemaphoreType.DMA((5,)),
        pltpu.SemaphoreType.DMA((4,)),
        pltpu.SemaphoreType.DMA((6,)),
        pltpu.SemaphoreType.DMA((Z,)),
    ]
    return pl.pallas_call(
        kernel,
        out_shape=(
            jax.ShapeDtypeStruct((2, 12, 8, 32), F32),
            jax.ShapeDtypeStruct((6, 8, 8), F32),
            jax.ShapeDtypeStruct((6, 2, 8), F32),
        ),
        in_specs=[hbm] * 5,
        out_specs=(vmem, vmem, vmem),
        scratch_shapes=scratch,
        compiler_params=pltpu.CompilerParams(
            collective_id=0, has_side_effects=True, vmem_limit_bytes=40 * 1024 * 1024
        ),
    )(*(pltpu.with_memory_space_constraint(x, pltpu.HBM) for x in (coherency, observed, flags, tile_map, jones)))


def solution(mesh):
    return jax.shard_map(
        body,
        mesh=mesh,
        in_specs=(
            P("tile", "dir", None, None, None),
            P("tile", None, None, None),
            P("tile", None),
            P("tile", None),
            P("dir", None, "tile"),
        ),
        out_specs=(P("tile", None, None, "dir"), P("dir", None, "tile"), P("dir", None, "tile")),
        check_vma=False,
    )
```

```python
import functools

import jax
import jax.numpy as jnp
from jax import lax
from jax.experimental import pallas as pl
from jax.experimental.pallas import tpu as pltpu
from jax.sharding import PartitionSpec as P

MESH = pl.DeviceIdType.MESH
YH, Z, CORES, DIRS = 4, 8, 2, 8
TILES = YH * Z * CORES
SB = 16
F32 = jnp.float32
BF16 = jnp.bfloat16


def hops(offset):
    y, z, c = offset
    return 2 * min(y, YH - y) + min(z, Z - z) + 0.5 * c


FAR_FIRST = sorted(
    (
        (y, z, c)
        for y in range(YH)
        for z in range(Z)
        for c in range(CORES)
        if (y, z, c) != (0, 0, 0)
    ),
    key=lambda o: -hops(o),
)
Z_NEAR_FIRST = (1, 7, 2, 6, 3, 5, 4)
Z_FAR_FIRST = (4, 3, 5, 2, 6, 1, 7)
YC_FAR_FIRST = ((2, 1), (2, 0), (1, 1), (3, 1), (1, 0), (3, 0), (0, 1))


def times_adjoint(a, b):
    re, im = [], []
    for r in range(2):
        for c in range(2):
            x, y = None, None
            for m in range(2):
                ar, ai, br, bi = a[r * 2 + m], a[4 + r * 2 + m], b[c * 2 + m], b[4 + c * 2 + m]
                xr, xi = ar * br + ai * bi, ai * br - ar * bi
                x, y = (xr, xi) if x is None else (x + xr, y + xi)
            re.append(x)
            im.append(y)
    return re + im


def times(a, b):
    re, im = [], []
    for r in range(2):
        for c in range(2):
            x, y = None, None
            for m in range(2):
                ar, ai, br, bi = a[r * 2 + m], a[4 + r * 2 + m], b[m * 2 + c], b[4 + m * 2 + c]
                xr, xi = ar * br - ai * bi, ar * bi + ai * br
                x, y = (xr, xi) if x is None else (x + xr, y + xi)
            re.append(x)
            im.append(y)
    return re + im


def adjoint_times(a, b):
    re, im = [], []
    for r in range(2):
        for c in range(2):
            x, y = None, None
            for m in range(2):
                ar, ai, br, bi = a[m * 2 + r], a[4 + m * 2 + r], b[m * 2 + c], b[4 + m * 2 + c]
                xr, xi = ar * br + ai * bi, ar * bi - ai * br
                x, y = (xr, xi) if x is None else (x + xr, y + xi)
            re.append(x)
            im.append(y)
    return re + im


def fold(values):
    row = lax.broadcasted_iota(jnp.int32, (8, 128), 0)
    first, even = row % 4 < 2, row % 2 == 0
    a, b, c, d = values
    e = jnp.where(first, a, pltpu.roll(c, 2, 0)) + jnp.where(first, pltpu.roll(a, 6, 0), c)
    f = jnp.where(first, b, pltpu.roll(d, 2, 0)) + jnp.where(first, pltpu.roll(b, 6, 0), d)
    return jnp.where(even, e, pltpu.roll(f, 1, 0)) + jnp.where(even, pltpu.roll(e, 7, 0), f)


def row_of(t, s):
    return s // 4 * 8 + t * 4 + s % 4


def split(x):
    high = x.astype(BF16)
    return high, (x - high.astype(F32)).astype(BF16)


def kernel(
    coherency,
    observed,
    flags_in,
    tile_map_in,
    jones_in,
    stage,
    owned,
    coh_raw,
    obs_raw,
    rows,
    obs_rows,
    coh,
    gains,
    m_all,
    n_all,
    partial,
    taken,
    residual,
    weight,
    val_p,
    val_q,
    pay,
    paid,
    jones_all,
    collect,
    flags,
    tile_map,
    jones,
    local_sem,
    send_sem,
    recv_sem,
    near_sem,
):
    tile, me = lax.axis_index("tile"), lax.axis_index("dir")
    y, z, core = tile // (Z * CORES), tile // CORES % Z, tile % CORES

    def at(dy, dz, dc):
        return (
            lax.rem(y + dy, YH) * (Z * CORES)
            + lax.rem(z + dz, Z) * CORES
            + lax.rem(core + dc, CORES)
        )

    def remote(src, dst, send, recv, device):
        return pltpu.make_async_remote_copy(
            src_ref=src,
            dst_ref=dst,
            send_sem=send,
            recv_sem=recv,
            device_id=device,
            device_id_type=MESH,
        )

    barrier = pltpu.get_barrier_semaphore()
    greeted = (
        [(at(0, dz, 0), me) for dz in Z_FAR_FIRST]
        + [(at(dy, 0, dc), me) for dy, dc in YC_FAR_FIRST]
        + [(tile, lax.rem(me + r, DIRS)) for r in range(1, DIRS)]
    )
    for device in greeted:
        pl.semaphore_signal(barrier, inc=1, device_id=device, device_id_type=MESH)

    here = [
        pltpu.make_async_copy(src, dst, local_sem.at[number])
        for number, (src, dst) in enumerate(
            (
                (jones_in, jones),
                (flags_in, flags),
                (tile_map_in, tile_map),
                (coherency, coh_raw),
                (observed, obs_raw),
            )
        )
    ]
    for copy in here:
        copy.start()

    here[0].wait()
    packed = jnp.zeros((8, 128), F32)
    for k in range(6):
        wide = jnp.concatenate([jones[k], jnp.zeros((8, 120), F32)], axis=1)
        packed = packed + (pltpu.roll(wide, 8 * k, 1) if k else wide)
    packed = packed[0:4] + pltpu.roll(packed, 64, 1)[4:8]
    jones_all[tile] = packed

    pl.semaphore_wait(barrier, len(greeted))

    mine = jones_all.at[tile]
    for dz in Z_FAR_FIRST:
        remote(mine, mine, send_sem.at[0], near_sem.at[dz], (at(0, dz, 0), me)).start()
    for dy, dc in YC_FAR_FIRST:
        remote(mine, mine, send_sem.at[0], recv_sem.at[0], (at(dy, 0, dc), me)).start()
    for copy in here[1:]:
        copy.wait()

    def to_rows(k, carry):
        for t in range(2):
            for s in range(12):
                block = coh_raw[t, k, s].astype(F32)
                for h in range(2):
                    rows[h, k, pl.ds(row_of(t, s) * 8, 8), :] = block[:, h * 128 : h * 128 + 128]
        for h in range(2):
            for c in range(8):
                coh[k, h, c] = rows[h, k, pl.ds(c, 24, stride=8), :].reshape(3, 8, 128)
        return carry

    lax.fori_loop(0, 6, to_rows, 0)
    for t in range(2):
        for s in range(12):
            block = obs_raw[t, s].astype(F32)
            for h in range(2):
                obs_rows[h, pl.ds(row_of(t, s) * 8, 8), :] = block[:, h * 128 : h * 128 + 128]

    second = lax.broadcasted_iota(jnp.int32, (8, 128), 0) >= 4
    for h in range(2):
        baseline = lax.broadcasted_iota(jnp.int32, (8, 128), 1) + 128 * h
        upper = jnp.where(baseline // SB < baseline % SB, 1, 0)
        for g in range(3):
            both = []
            for t in range(2):
                ahead = jnp.where(tile_map[t, 0] < tile_map[t, 1], 1, 0)
                kept = 1 - flags[t, g]
                both.append((jnp.maximum(upper, ahead) * kept).astype(F32))
            weight[h, g] = jnp.where(second, both[1], both[0])

    baseline = lax.broadcasted_iota(jnp.int32, (256, 256), 0)
    station = lax.broadcasted_iota(jnp.int32, (256, 256), 1)
    station = station // 128 * 8 + station % 8
    for side in range(2):
        own = station == (baseline % SB if side else baseline // SB)
        collect[side] = jnp.where(own, 1.0, 0.0).astype(BF16)
    val_p[15] = jnp.zeros((8, 256), F32)
    val_q[15] = jnp.zeros((8, 256), F32)

    for dz in Z_NEAR_FIRST:
        piece = jones_all.at[at(0, Z - dz, 0)]
        remote(piece, piece, send_sem.at[0], near_sem.at[dz], (at(0, dz, 0), me)).wait_recv()
        for dy, dc in YC_FAR_FIRST:
            remote(piece, piece, send_sem.at[0], recv_sem.at[0], (at(dy, 0, dc), me)).start()
    count = 7 * Z
    far = jones_all.at[pl.ds(0, count)]
    remote(far, far, send_sem.at[0], recv_sem.at[0], (at(1, 0, 0), me)).wait_recv()

    row = lax.broadcasted_iota(jnp.int32, (6, 8, 256), 1)
    direction = lax.broadcasted_iota(jnp.int32, (6, 8, 256), 0)
    lane = lax.broadcasted_iota(jnp.int32, (6, 8, 256), 2)
    own = lane % 128 // 8 == row // 4 * 8 + direction
    station = lax.broadcasted_iota(jnp.int32, (256, 256), 0)
    station = station // 128 * 8 + station % 8
    baseline = lax.broadcasted_iota(jnp.int32, (256, 256), 1)
    for side in range(2):
        spread = jnp.where(station == (baseline % SB if side else baseline // SB), 1.0, 0.0)
        spread = spread.astype(BF16)
        for t in range(2):
            block = tile_map[t, side]
            both = jnp.concatenate([jones_all[2 * block], jones_all[2 * block + 1]], axis=1)
            both = jnp.concatenate([both, both], axis=0)
            chosen = jnp.where(own, both[None], 0.0).reshape(48, 256)
            high, low = split(chosen)
            full = jnp.dot(high, spread, preferred_element_type=F32)
            full = full + jnp.dot(low, spread, preferred_element_type=F32)
            for h in range(2):
                gains[side, t, h] = full[:, h * 128 : h * 128 + 128].reshape(6, 8, 128)

    def gain(side, k, h):
        return [
            jnp.where(
                second,
                jnp.broadcast_to(gains[side, 1, h, k, pl.ds(c, 1), :], (8, 128)),
                jnp.broadcast_to(gains[side, 0, h, k, pl.ds(c, 1), :], (8, 128)),
            )
            for c in range(8)
        ]

    for h in range(2):

        def add_direction(k, total, h=h):
            p, q = gain(0, k, h), gain(1, k, h)
            out = []
            for g in range(3):
                m = times_adjoint([coh[k, h, c, g] for c in range(8)], q)
                for c in range(8):
                    m_all[k, h, c, g] = m[c]
                v = times(p, m)
                out += [total[g * 8 + c] + v[c] for c in range(8)]
            return tuple(out)

        total = lax.fori_loop(0, 6, add_direction, (jnp.zeros((8, 128), F32),) * 24)
        for g in range(3):
            for c in range(8):
                partial[c, h, g] = total[g * 8 + c]

        for r in range(1, DIRS):
            other = lax.rem(me + r, DIRS)
            remote(
                partial.at[other, h],
                taken.at[h, r - 1],
                send_sem.at[1],
                recv_sem.at[1 + h],
                (tile, other),
            ).start()

    for h in range(2):

        def two_directions(pair, carry, h=h):
            rows_p, rows_q = [], []
            for j in range(2):
                k = pair * 2 + j
                p = gain(0, k, h)
                cp, cq = [0.0, 0.0], [0.0, 0.0]
                for g in range(3):
                    n = times(p, [coh[k, h, c, g] for c in range(8)])
                    for c in range(8):
                        n_all[k, h, c, g] = n[c]
                    m = [m_all[k, h, c, g] for c in range(8)]
                    w = weight[h, g]
                    for c in range(2):
                        cp[c] = cp[c] + w * sum(m[e] * m[e] for e in (2 * c, 2 * c + 1, 4 + 2 * c, 5 + 2 * c))
                        cq[c] = cq[c] + w * sum(n[e] * n[e] for e in (c, c + 2, c + 4, c + 6))
                rows_p += cp
                rows_q += cq
            val_p[12 + pair, :, h * 128 : h * 128 + 128] = fold(rows_p)
            val_q[12 + pair, :, h * 128 : h * 128 + 128] = fold(rows_q)
            return carry

        lax.fori_loop(0, 3, two_directions, 0)

    for h in range(2):
        got = taken.at[h]
        remote(got, got, send_sem.at[1], recv_sem.at[1 + h], (tile, me)).wait_recv()
        model = partial[me, h]
        for r in range(DIRS - 1):
            model = model + taken[h, r]
        seen = obs_rows[h, pl.ds(me, 24, stride=8), :].reshape(3, 8, 128)
        residual[h, me] = weight[h] * (seen - model)
        done = residual.at[h, me]
        for r in range(1, DIRS):
            other = lax.rem(me + r, DIRS)
            remote(done, done, send_sem.at[2], recv_sem.at[3 + h], (tile, other)).start()

    for h in range(2):
        got = residual.at[h, pl.ds(0, DIRS - 1)]
        remote(got, got, send_sem.at[2], recv_sem.at[3 + h], (tile, me)).wait_recv()

        def one_direction(k, carry, h=h):
            a, b = None, None
            for g in range(3):
                res = [residual[h, c, g] for c in range(8)]
                u = times_adjoint(res, [m_all[k, h, c, g] for c in range(8)])
                v = adjoint_times(res, [n_all[k, h, c, g] for c in range(8)])
                a = u if a is None else [i + j for i, j in zip(a, u)]
                b = v if b is None else [i + j for i, j in zip(b, v)]
            for j in range(2):
                val_p[2 * k + j, :, h * 128 : h * 128 + 128] = fold(a[4 * j : 4 * j + 4])
                val_q[2 * k + j, :, h * 128 : h * 128 + 128] = fold(b[4 * j : 4 * j + 4])
            return carry

        lax.fori_loop(0, 6, one_direction, 0)

    group = lax.broadcasted_iota(jnp.int32, (8, 128), 1) // 8
    parts = []
    for side, val in ((0, val_p), (1, val_q)):
        high, low = split(val[...].reshape(128, 256))
        sums = jnp.dot(high, collect[side], preferred_element_type=F32)
        sums = sums + jnp.dot(low, collect[side], preferred_element_type=F32)
        sums = sums.reshape(16, 8, 256)
        halves = []
        for h in range(2):
            piece = jnp.zeros((8, 128), F32)
            for g in range(15):
                piece = jnp.where(group == g, sums[g, :, h * 128 : h * 128 + 128], piece)
            halves.append(piece)
        parts.append((side, 0, jnp.where(second, pltpu.roll(halves[1], 4, 0), halves[0])))
        parts.append((side, 1, jnp.where(second, halves[1], pltpu.roll(halves[0], 4, 0))))

    for b in range(TILES // 2):
        block = jnp.zeros((8, 128), F32)
        for side, t, part in parts:
            block = block + jnp.where(tile_map[t, side] == b, part, 0.0)
        pay[2 * b] = block[0:4]
        pay[2 * b + 1] = block[4:8]

    for number, (dy, dz, dc) in enumerate(FAR_FIRST):
        owner = at(dy, dz, dc)
        remote(
            pay.at[owner], paid.at[number], send_sem.at[3], recv_sem.at[5], (owner, me)
        ).start()

    half, part = me // 4, me % 4
    for c in range(8):
        wide = residual[half, c].reshape(24, 128)
        wide = pltpu.roll(wide, lax.rem(128 - 32 * part, 128), 1)
        stage[pl.ds(c, 24, stride=8), :] = wide

    remote(paid, paid, send_sem.at[3], recv_sem.at[5], (tile, me)).wait_recv()
    terms = [pay[tile]] + [paid[number] for number in range(TILES - 1)]
    while len(terms) > 1:
        terms = [a + b for a, b in zip(terms[::2], terms[1::2])]
    owned[...] = terms[0] * (1.0 / (12 * SB))

    sent = jones_all.at[pl.ds(0, TILES - 1)]
    remote(sent, sent, send_sem.at[0], recv_sem.at[0], (tile, me)).wait_send()
    remote(taken, taken, send_sem.at[1], recv_sem.at[1], (tile, me)).wait_send()
    remote(taken, taken, send_sem.at[2], recv_sem.at[1], (tile, me)).wait_send()
    remote(paid, paid, send_sem.at[3], recv_sem.at[5], (tile, me)).wait_send()


def unpack(stage, owned, res_out, grad_out, curv_out, res, grad, curv, sem):
    total = owned[...]
    moved = [(pltpu.roll(total, 128 - 8 * g, 1) if g else total)[:, 0:8] for g in range(15)]
    for k in range(6):
        grad[k] = jnp.concatenate(moved[2 * k : 2 * k + 2], axis=0)
        curv[k] = moved[12 + k // 2][k % 2 * 2 : k % 2 * 2 + 2]
    for t in range(2):
        for s in range(12):
            res[t, s] = stage[pl.ds(row_of(t, s) * 8, 8), 0:32]
    copies = [
        pltpu.make_async_copy(src, dst, sem.at[number])
        for number, (src, dst) in enumerate(((res, res_out), (grad, grad_out), (curv, curv_out)))
    ]
    for copy in copies:
        copy.start()
    for copy in copies:
        copy.wait()


def body(coherency, observed, flags, tile_map, jones):
    vmem, hbm = (pl.BlockSpec(memory_space=m) for m in (pltpu.VMEM, pltpu.HBM))
    scratch = [
        pltpu.VMEM((2, 6, 12, 8, 256), BF16),
        pltpu.VMEM((2, 12, 8, 256), BF16),
        pltpu.VMEM((2, 6, 192, 128), F32),
        pltpu.VMEM((2, 192, 128), F32),
        pltpu.VMEM((6, 2, 8, 3, 8, 128), F32),
        pltpu.VMEM((2, 2, 2, 6, 8, 128), F32),
        pltpu.VMEM((6, 2, 8, 3, 8, 128), F32),
        pltpu.VMEM((6, 2, 8, 3, 8, 128), F32),
        pltpu.VMEM((8, 2, 3, 8, 128), F32),
        pltpu.VMEM((2, 7, 3, 8, 128), F32),
        pltpu.VMEM((2, 8, 3, 8, 128), F32),
        pltpu.VMEM((2, 3, 8, 128), F32),
        pltpu.VMEM((16, 8, 256), F32),
        pltpu.VMEM((16, 8, 256), F32),
        pltpu.VMEM((TILES, 4, 128), F32),
        pltpu.VMEM((TILES - 1, 4, 128), F32),
        pltpu.VMEM((TILES, 4, 128), F32),
        pltpu.VMEM((2, 256, 256), BF16),
        pltpu.SMEM((2, 3), jnp.int32),
        pltpu.SMEM((2, 2), jnp.int32),
        pltpu.VMEM((6, 8, 8), F32),
        pltpu.SemaphoreType.DMA((5,)),
        pltpu.SemaphoreType.DMA((4,)),
        pltpu.SemaphoreType.DMA((6,)),
        pltpu.SemaphoreType.DMA((Z,)),
    ]
    summed = pl.pallas_call(
        kernel,
        out_shape=(
            jax.ShapeDtypeStruct((192, 128), F32),
            jax.ShapeDtypeStruct((4, 128), F32),
        ),
        in_specs=[hbm] * 5,
        out_specs=(vmem, vmem),
        scratch_shapes=scratch,
        compiler_params=pltpu.CompilerParams(
            collective_id=0, has_side_effects=True, vmem_limit_bytes=40 * 1024 * 1024
        ),
    )(*(pltpu.with_memory_space_constraint(x, pltpu.HBM) for x in (coherency, observed, flags, tile_map, jones)))
    shapes = ((2, 12, 8, 32), (6, 8, 8), (6, 2, 8))
    return pl.pallas_call(
        unpack,
        out_shape=tuple(jax.ShapeDtypeStruct(shape, F32) for shape in shapes),
        in_specs=[vmem, vmem],
        out_specs=(hbm, hbm, hbm),
        scratch_shapes=[pltpu.VMEM(shape, F32) for shape in shapes] + [pltpu.SemaphoreType.DMA((3,))],
        compiler_params=pltpu.CompilerParams(vmem_limit_bytes=8 * 1024 * 1024),
    )(*summed)


def solution(mesh):
    return jax.shard_map(
        body,
        mesh=mesh,
        in_specs=(
            P("tile", "dir", None, None, None),
            P("tile", None, None, None),
            P("tile", None),
            P("tile", None),
            P("dir", None, "tile"),
        ),
        out_specs=(P("tile", None, None, "dir"), P("dir", None, "tile"), P("dir", None, "tile")),
        check_vma=False,
    )
```

```python
import functools

import jax
import jax.numpy as jnp
from jax import lax
from jax.experimental import pallas as pl
from jax.experimental.pallas import tpu as pltpu
from jax.sharding import PartitionSpec as P

MESH = pl.DeviceIdType.MESH
YH, Z, CORES, DIRS = 4, 8, 2, 8
TILES = YH * Z * CORES
SB = 16
F32 = jnp.float32
BF16 = jnp.bfloat16


def hops(offset):
    y, z, c = offset
    return 2 * min(y, YH - y) + min(z, Z - z) + 0.5 * c


FAR_FIRST = sorted(
    (
        (y, z, c)
        for y in range(YH)
        for z in range(Z)
        for c in range(CORES)
        if (y, z, c) != (0, 0, 0)
    ),
    key=lambda o: -hops(o),
)
Z_NEAR_FIRST = (1, 7, 2, 6, 3, 5, 4)
Z_FAR_FIRST = (4, 3, 5, 2, 6, 1, 7)
DIR_FAR_FIRST = ((2, 1), (2, 0), (1, 1), (3, 1), (1, 0), (3, 0), (0, 1))
YC_FAR_FIRST = ((2, 1), (2, 0), (1, 1), (3, 1), (1, 0), (3, 0), (0, 1))


def times_adjoint(a, b):
    re, im = [], []
    for r in range(2):
        for c in range(2):
            x, y = None, None
            for m in range(2):
                ar, ai, br, bi = a[r * 2 + m], a[4 + r * 2 + m], b[c * 2 + m], b[4 + c * 2 + m]
                xr, xi = ar * br + ai * bi, ai * br - ar * bi
                x, y = (xr, xi) if x is None else (x + xr, y + xi)
            re.append(x)
            im.append(y)
    return re + im


def times(a, b):
    re, im = [], []
    for r in range(2):
        for c in range(2):
            x, y = None, None
            for m in range(2):
                ar, ai, br, bi = a[r * 2 + m], a[4 + r * 2 + m], b[m * 2 + c], b[4 + m * 2 + c]
                xr, xi = ar * br - ai * bi, ar * bi + ai * br
                x, y = (xr, xi) if x is None else (x + xr, y + xi)
            re.append(x)
            im.append(y)
    return re + im


def adjoint_times(a, b):
    re, im = [], []
    for r in range(2):
        for c in range(2):
            x, y = None, None
            for m in range(2):
                ar, ai, br, bi = a[m * 2 + r], a[4 + m * 2 + r], b[m * 2 + c], b[4 + m * 2 + c]
                xr, xi = ar * br + ai * bi, ar * bi - ai * br
                x, y = (xr, xi) if x is None else (x + xr, y + xi)
            re.append(x)
            im.append(y)
    return re + im


def fold(values):
    row = lax.broadcasted_iota(jnp.int32, (8, 128), 0)
    first, even = row % 4 < 2, row % 2 == 0
    a, b, c, d = values
    e = jnp.where(first, a, pltpu.roll(c, 2, 0)) + jnp.where(first, pltpu.roll(a, 6, 0), c)
    f = jnp.where(first, b, pltpu.roll(d, 2, 0)) + jnp.where(first, pltpu.roll(b, 6, 0), d)
    return jnp.where(even, e, pltpu.roll(f, 1, 0)) + jnp.where(even, pltpu.roll(e, 7, 0), f)


def row_of(t, s):
    return s // 4 * 8 + t * 4 + s % 4


def split(x):
    high = x.astype(BF16)
    return high, (x - high.astype(F32)).astype(BF16)


def kernel(
    coherency,
    observed,
    flags_in,
    tile_map_in,
    jones_in,
    stage,
    owned,
    coh_raw,
    obs_raw,
    rows,
    obs_rows,
    coh,
    gains,
    m_all,
    n_all,
    partial,
    taken,
    residual,
    weight,
    val_p,
    val_q,
    pay,
    paid,
    jones_all,
    collect,
    spread,
    chosen_lane,
    flags,
    tile_map,
    jones,
    local_sem,
    send_sem,
    recv_sem,
    near_sem,
):
    tile, me = lax.axis_index("tile"), lax.axis_index("dir")
    y, z, core = tile // (Z * CORES), tile // CORES % Z, tile % CORES

    def at(dy, dz, dc):
        return (
            lax.rem(y + dy, YH) * (Z * CORES)
            + lax.rem(z + dz, Z) * CORES
            + lax.rem(core + dc, CORES)
        )

    def along_dir(dx, dl):
        return lax.rem(me // 2 + dx, DIRS // 2) * 2 + lax.rem(me + dl, 2)

    def remote(src, dst, send, recv, device):
        return pltpu.make_async_remote_copy(
            src_ref=src,
            dst_ref=dst,
            send_sem=send,
            recv_sem=recv,
            device_id=device,
            device_id_type=MESH,
        )

    barrier = pltpu.get_barrier_semaphore()
    greeted = (
        [(at(0, dz, 0), me) for dz in Z_FAR_FIRST]
        + [(at(dy, 0, dc), me) for dy, dc in YC_FAR_FIRST]
        + [(tile, along_dir(dx, dl)) for dx, dl in DIR_FAR_FIRST]
    )
    for device in greeted:
        pl.semaphore_signal(barrier, inc=1, device_id=device, device_id_type=MESH)

    here = [
        pltpu.make_async_copy(src, dst, local_sem.at[number])
        for number, (src, dst) in enumerate(
            (
                (jones_in, jones),
                (flags_in, flags),
                (tile_map_in, tile_map),
                (coherency, coh_raw),
                (observed, obs_raw),
            )
        )
    ]
    for copy in here:
        copy.start()

    here[0].wait()
    packed = jnp.zeros((8, 128), F32)
    for k in range(6):
        wide = jnp.concatenate([jones[k], jnp.zeros((8, 120), F32)], axis=1)
        packed = packed + (pltpu.roll(wide, 8 * k, 1) if k else wide)
    packed = packed[0:4] + pltpu.roll(packed, 64, 1)[4:8]
    jones_all[tile] = packed

    pl.semaphore_wait(barrier, len(greeted))

    mine = jones_all.at[tile]
    for dz in Z_FAR_FIRST:
        remote(mine, mine, send_sem.at[0], near_sem.at[dz], (at(0, dz, 0), me)).start()
    for dy, dc in YC_FAR_FIRST:
        remote(mine, mine, send_sem.at[0], recv_sem.at[0], (at(dy, 0, dc), me)).start()
    for copy in here[1:]:
        copy.wait()

    def to_rows(k, carry):
        for t in range(2):
            for s in range(12):
                block = coh_raw[t, k, s].astype(F32)
                for h in range(2):
                    rows[h, k, pl.ds(row_of(t, s) * 8, 8), :] = block[:, h * 128 : h * 128 + 128]
        for h in range(2):
            for c in range(8):
                coh[k, h, c] = rows[h, k, pl.ds(c, 24, stride=8), :].reshape(3, 8, 128)
        return carry

    lax.fori_loop(0, 6, to_rows, 0)
    for t in range(2):
        for s in range(12):
            block = obs_raw[t, s].astype(F32)
            for h in range(2):
                obs_rows[h, pl.ds(row_of(t, s) * 8, 8), :] = block[:, h * 128 : h * 128 + 128]

    second = lax.broadcasted_iota(jnp.int32, (8, 128), 0) >= 4
    for h in range(2):
        baseline = lax.broadcasted_iota(jnp.int32, (8, 128), 1) + 128 * h
        upper = jnp.where(baseline // SB < baseline % SB, 1, 0)
        for g in range(3):
            both = []
            for t in range(2):
                ahead = jnp.where(tile_map[t, 0] < tile_map[t, 1], 1, 0)
                kept = 1 - flags[t, g]
                both.append((jnp.maximum(upper, ahead) * kept).astype(F32))
            weight[h, g] = jnp.where(second, both[1], both[0])

    row = lax.broadcasted_iota(jnp.int32, (6, 8, 256), 1)
    direction = lax.broadcasted_iota(jnp.int32, (6, 8, 256), 0)
    lane = lax.broadcasted_iota(jnp.int32, (6, 8, 256), 2)
    chosen_lane[...] = jnp.where(lane % 128 // 8 == row // 4 * 8 + direction, 1.0, 0.0)
    station = lax.broadcasted_iota(jnp.int32, (256, 256), 0)
    station = station // 128 * 8 + station % 8
    baseline = lax.broadcasted_iota(jnp.int32, (256, 256), 1)
    for side in range(2):
        takes = station == (baseline % SB if side else baseline // SB)
        spread[side] = jnp.where(takes, 1.0, 0.0).astype(BF16)
    baseline = lax.broadcasted_iota(jnp.int32, (256, 256), 0)
    station = lax.broadcasted_iota(jnp.int32, (256, 256), 1)
    station = station // 128 * 8 + station % 8
    for side in range(2):
        own = station == (baseline % SB if side else baseline // SB)
        collect[side] = jnp.where(own, 1.0, 0.0).astype(BF16)
    val_p[15] = jnp.zeros((8, 256), F32)
    val_q[15] = jnp.zeros((8, 256), F32)

    for dz in Z_NEAR_FIRST:
        piece = jones_all.at[at(0, Z - dz, 0)]
        remote(piece, piece, send_sem.at[0], near_sem.at[dz], (at(0, dz, 0), me)).wait_recv()
        for dy, dc in YC_FAR_FIRST:
            remote(piece, piece, send_sem.at[0], recv_sem.at[0], (at(dy, 0, dc), me)).start()
    count = 7 * Z
    far = jones_all.at[pl.ds(0, count)]
    remote(far, far, send_sem.at[0], recv_sem.at[0], (at(1, 0, 0), me)).wait_recv()

    mask = chosen_lane[...]
    for side in range(2):
        picked = []
        for t in range(2):
            block = tile_map[t, side]
            both = jnp.concatenate([jones_all[2 * block], jones_all[2 * block + 1]], axis=1)
            both = jnp.concatenate([both, both], axis=0)
            picked.append(jnp.where(mask != 0.0, both[None], 0.0).reshape(48, 256))
        high, low = split(jnp.concatenate(picked, axis=0))
        full = jnp.dot(
            jnp.concatenate([high, low], axis=0), spread[side], preferred_element_type=F32
        )
        full = full[0:96] + full[96:192]
        for t in range(2):
            for h in range(2):
                block = full[t * 48 : t * 48 + 48, h * 128 : h * 128 + 128]
                gains[side, t, h] = block.reshape(6, 8, 128)

    def gain(side, k, h):
        return [
            jnp.where(
                second,
                jnp.broadcast_to(gains[side, 1, h, k, pl.ds(c, 1), :], (8, 128)),
                jnp.broadcast_to(gains[side, 0, h, k, pl.ds(c, 1), :], (8, 128)),
            )
            for c in range(8)
        ]

    for h in range(2):

        def add_direction(k, total, h=h):
            p, q = gain(0, k, h), gain(1, k, h)
            out = []
            for g in range(3):
                m = times_adjoint([coh[k, h, c, g] for c in range(8)], q)
                for c in range(8):
                    m_all[k, h, c, g] = m[c]
                v = times(p, m)
                out += [total[g * 8 + c] + v[c] for c in range(8)]
            return tuple(out)

        total = lax.fori_loop(0, 6, add_direction, (jnp.zeros((8, 128), F32),) * 24)
        for g in range(3):
            for c in range(8):
                partial[c, h, g] = total[g * 8 + c]

        for number, (dx, dl) in enumerate(DIR_FAR_FIRST):
            other = along_dir(dx, dl)
            remote(
                partial.at[other, h],
                taken.at[h, number],
                send_sem.at[1],
                recv_sem.at[1 + h],
                (tile, other),
            ).start()

    for h in range(2):

        def two_directions(pair, carry, h=h):
            rows_p, rows_q = [], []
            for j in range(2):
                k = pair * 2 + j
                p = gain(0, k, h)
                cp, cq = [0.0, 0.0], [0.0, 0.0]
                for g in range(3):
                    n = times(p, [coh[k, h, c, g] for c in range(8)])
                    for c in range(8):
                        n_all[k, h, c, g] = n[c]
                    m = [m_all[k, h, c, g] for c in range(8)]
                    w = weight[h, g]
                    for c in range(2):
                        cp[c] = cp[c] + w * sum(m[e] * m[e] for e in (2 * c, 2 * c + 1, 4 + 2 * c, 5 + 2 * c))
                        cq[c] = cq[c] + w * sum(n[e] * n[e] for e in (c, c + 2, c + 4, c + 6))
                rows_p += cp
                rows_q += cq
            val_p[12 + pair, :, h * 128 : h * 128 + 128] = fold(rows_p)
            val_q[12 + pair, :, h * 128 : h * 128 + 128] = fold(rows_q)
            return carry

        lax.fori_loop(0, 3, two_directions, 0)

    for h in range(2):
        got = taken.at[h]
        remote(got, got, send_sem.at[1], recv_sem.at[1 + h], (tile, me)).wait_recv()
        model = partial[me, h]
        for r in range(DIRS - 1):
            model = model + taken[h, r]
        seen = obs_rows[h, pl.ds(me, 24, stride=8), :].reshape(3, 8, 128)
        residual[h, me] = weight[h] * (seen - model)
        done = residual.at[h, me]
        for dx, dl in DIR_FAR_FIRST:
            other = along_dir(dx, dl)
            remote(done, done, send_sem.at[2], recv_sem.at[3 + h], (tile, other)).start()

    for h in range(2):
        got = residual.at[h, pl.ds(0, DIRS - 1)]
        remote(got, got, send_sem.at[2], recv_sem.at[3 + h], (tile, me)).wait_recv()

        def one_direction(k, carry, h=h):
            a, b = None, None
            for g in range(3):
                res = [residual[h, c, g] for c in range(8)]
                u = times_adjoint(res, [m_all[k, h, c, g] for c in range(8)])
                v = adjoint_times(res, [n_all[k, h, c, g] for c in range(8)])
                a = u if a is None else [i + j for i, j in zip(a, u)]
                b = v if b is None else [i + j for i, j in zip(b, v)]
            for j in range(2):
                val_p[2 * k + j, :, h * 128 : h * 128 + 128] = fold(a[4 * j : 4 * j + 4])
                val_q[2 * k + j, :, h * 128 : h * 128 + 128] = fold(b[4 * j : 4 * j + 4])
            return carry

        lax.fori_loop(0, 6, one_direction, 0)

    group = lax.broadcasted_iota(jnp.int32, (8, 128), 1) // 8
    parts = []
    for side, val in ((0, val_p), (1, val_q)):
        high, low = split(val[...].reshape(128, 256))
        sums = jnp.dot(
            jnp.concatenate([high, low], axis=0), collect[side], preferred_element_type=F32
        )
        sums = (sums[0:128] + sums[128:256]).reshape(16, 8, 256)
        halves = []
        for h in range(2):
            piece = jnp.zeros((8, 128), F32)
            for g in range(15):
                piece = jnp.where(group == g, sums[g, :, h * 128 : h * 128 + 128], piece)
            halves.append(piece)
        parts.append((side, 0, jnp.where(second, pltpu.roll(halves[1], 4, 0), halves[0])))
        parts.append((side, 1, jnp.where(second, halves[1], pltpu.roll(halves[0], 4, 0))))

    for b in range(TILES // 2):
        block = jnp.zeros((8, 128), F32)
        for side, t, part in parts:
            block = block + jnp.where(tile_map[t, side] == b, part, 0.0)
        pay[2 * b] = block[0:4]
        pay[2 * b + 1] = block[4:8]

    for number, (dy, dz, dc) in enumerate(FAR_FIRST):
        owner = at(dy, dz, dc)
        remote(
            pay.at[owner], paid.at[number], send_sem.at[3], recv_sem.at[5], (owner, me)
        ).start()

    half, part = me // 4, me % 4
    for c in range(8):
        wide = residual[half, c].reshape(24, 128)
        wide = pltpu.roll(wide, lax.rem(128 - 32 * part, 128), 1)
        stage[pl.ds(c, 24, stride=8), :] = wide

    remote(paid, paid, send_sem.at[3], recv_sem.at[5], (tile, me)).wait_recv()
    terms = [pay[tile]] + [paid[number] for number in range(TILES - 1)]
    while len(terms) > 1:
        terms = [a + b for a, b in zip(terms[::2], terms[1::2])]
    owned[...] = terms[0] * (1.0 / (12 * SB))

    sent = jones_all.at[pl.ds(0, TILES - 1)]
    remote(sent, sent, send_sem.at[0], recv_sem.at[0], (tile, me)).wait_send()
    remote(taken, taken, send_sem.at[1], recv_sem.at[1], (tile, me)).wait_send()
    remote(taken, taken, send_sem.at[2], recv_sem.at[1], (tile, me)).wait_send()
    remote(paid, paid, send_sem.at[3], recv_sem.at[5], (tile, me)).wait_send()


def unpack(stage, owned, res_out, grad_out, curv_out, res, grad, curv, sem):
    total = owned[...]
    moved = [(pltpu.roll(total, 128 - 8 * g, 1) if g else total)[:, 0:8] for g in range(15)]
    for k in range(6):
        grad[k] = jnp.concatenate(moved[2 * k : 2 * k + 2], axis=0)
        curv[k] = moved[12 + k // 2][k % 2 * 2 : k % 2 * 2 + 2]
    for t in range(2):
        for s in range(12):
            res[t, s] = stage[pl.ds(row_of(t, s) * 8, 8), 0:32]
    copies = [
        pltpu.make_async_copy(src, dst, sem.at[number])
        for number, (src, dst) in enumerate(((res, res_out), (grad, grad_out), (curv, curv_out)))
    ]
    for copy in copies:
        copy.start()
    for copy in copies:
        copy.wait()


def body(coherency, observed, flags, tile_map, jones):
    vmem, hbm = (pl.BlockSpec(memory_space=m) for m in (pltpu.VMEM, pltpu.HBM))
    scratch = [
        pltpu.VMEM((2, 6, 12, 8, 256), BF16),
        pltpu.VMEM((2, 12, 8, 256), BF16),
        pltpu.VMEM((2, 6, 192, 128), F32),
        pltpu.VMEM((2, 192, 128), F32),
        pltpu.VMEM((6, 2, 8, 3, 8, 128), F32),
        pltpu.VMEM((2, 2, 2, 6, 8, 128), F32),
        pltpu.VMEM((6, 2, 8, 3, 8, 128), F32),
        pltpu.VMEM((6, 2, 8, 3, 8, 128), F32),
        pltpu.VMEM((8, 2, 3, 8, 128), F32),
        pltpu.VMEM((2, 7, 3, 8, 128), F32),
        pltpu.VMEM((2, 8, 3, 8, 128), F32),
        pltpu.VMEM((2, 3, 8, 128), F32),
        pltpu.VMEM((16, 8, 256), F32),
        pltpu.VMEM((16, 8, 256), F32),
        pltpu.VMEM((TILES, 4, 128), F32),
        pltpu.VMEM((TILES - 1, 4, 128), F32),
        pltpu.VMEM((TILES, 4, 128), F32),
        pltpu.VMEM((2, 256, 256), BF16),
        pltpu.VMEM((2, 256, 256), BF16),
        pltpu.VMEM((6, 8, 256), F32),
        pltpu.SMEM((2, 3), jnp.int32),
        pltpu.SMEM((2, 2), jnp.int32),
        pltpu.VMEM((6, 8, 8), F32),
        pltpu.SemaphoreType.DMA((5,)),
        pltpu.SemaphoreType.DMA((4,)),
        pltpu.SemaphoreType.DMA((6,)),
        pltpu.SemaphoreType.DMA((Z,)),
    ]
    summed = pl.pallas_call(
        kernel,
        out_shape=(
            jax.ShapeDtypeStruct((192, 128), F32),
            jax.ShapeDtypeStruct((4, 128), F32),
        ),
        in_specs=[hbm] * 5,
        out_specs=(vmem, vmem),
        scratch_shapes=scratch,
        compiler_params=pltpu.CompilerParams(
            collective_id=0, has_side_effects=True, vmem_limit_bytes=40 * 1024 * 1024
        ),
    )(*(pltpu.with_memory_space_constraint(x, pltpu.HBM) for x in (coherency, observed, flags, tile_map, jones)))
    shapes = ((2, 12, 8, 32), (6, 8, 8), (6, 2, 8))
    return pl.pallas_call(
        unpack,
        out_shape=tuple(jax.ShapeDtypeStruct(shape, F32) for shape in shapes),
        in_specs=[vmem, vmem],
        out_specs=(hbm, hbm, hbm),
        scratch_shapes=[pltpu.VMEM(shape, F32) for shape in shapes] + [pltpu.SemaphoreType.DMA((3,))],
        compiler_params=pltpu.CompilerParams(vmem_limit_bytes=8 * 1024 * 1024),
    )(*summed)


def solution(mesh):
    return jax.shard_map(
        body,
        mesh=mesh,
        in_specs=(
            P("tile", "dir", None, None, None),
            P("tile", None, None, None),
            P("tile", None),
            P("tile", None),
            P("dir", None, "tile"),
        ),
        out_specs=(P("tile", None, None, "dir"), P("dir", None, "tile"), P("dir", None, "tile")),
        check_vma=False,
    )
```

```python
import functools

import jax
import jax.numpy as jnp
from jax import lax
from jax.experimental import pallas as pl
from jax.experimental.pallas import tpu as pltpu
from jax.sharding import PartitionSpec as P

MESH = pl.DeviceIdType.MESH
YH, Z, CORES, DIRS = 4, 8, 2, 8
TILES = YH * Z * CORES
SB = 16
F32 = jnp.float32
BF16 = jnp.bfloat16


def hops(offset):
    y, z, c = offset
    return 2 * min(y, YH - y) + min(z, Z - z) + 0.5 * c


FAR_FIRST = sorted(
    (
        (y, z, c)
        for y in range(YH)
        for z in range(Z)
        for c in range(CORES)
        if (y, z, c) != (0, 0, 0)
    ),
    key=lambda o: -hops(o),
)
Z_NEAR_FIRST = (1, 7, 2, 6, 3, 5, 4)
Z_FAR_FIRST = (4, 3, 5, 2, 6, 1, 7)
DIR_FAR_FIRST = ((2, 1), (2, 0), (1, 1), (3, 1), (1, 0), (3, 0), (0, 1))
YC_FAR_FIRST = ((2, 1), (2, 0), (1, 1), (3, 1), (1, 0), (3, 0), (0, 1))


def times_adjoint(a, b):
    re, im = [], []
    for r in range(2):
        for c in range(2):
            x, y = None, None
            for m in range(2):
                ar, ai, br, bi = a[r * 2 + m], a[4 + r * 2 + m], b[c * 2 + m], b[4 + c * 2 + m]
                xr, xi = ar * br + ai * bi, ai * br - ar * bi
                x, y = (xr, xi) if x is None else (x + xr, y + xi)
            re.append(x)
            im.append(y)
    return re + im


def times(a, b):
    re, im = [], []
    for r in range(2):
        for c in range(2):
            x, y = None, None
            for m in range(2):
                ar, ai, br, bi = a[r * 2 + m], a[4 + r * 2 + m], b[m * 2 + c], b[4 + m * 2 + c]
                xr, xi = ar * br - ai * bi, ar * bi + ai * br
                x, y = (xr, xi) if x is None else (x + xr, y + xi)
            re.append(x)
            im.append(y)
    return re + im


def adjoint_times(a, b):
    re, im = [], []
    for r in range(2):
        for c in range(2):
            x, y = None, None
            for m in range(2):
                ar, ai, br, bi = a[m * 2 + r], a[4 + m * 2 + r], b[m * 2 + c], b[4 + m * 2 + c]
                xr, xi = ar * br + ai * bi, ar * bi - ai * br
                x, y = (xr, xi) if x is None else (x + xr, y + xi)
            re.append(x)
            im.append(y)
    return re + im


def fold(values):
    row = lax.broadcasted_iota(jnp.int32, (8, 128), 0)
    first, even = row % 4 < 2, row % 2 == 0
    a, b, c, d = values
    e = jnp.where(first, a, pltpu.roll(c, 2, 0)) + jnp.where(first, pltpu.roll(a, 6, 0), c)
    f = jnp.where(first, b, pltpu.roll(d, 2, 0)) + jnp.where(first, pltpu.roll(b, 6, 0), d)
    return jnp.where(even, e, pltpu.roll(f, 1, 0)) + jnp.where(even, pltpu.roll(e, 7, 0), f)


def row_of(t, s):
    return s // 4 * 8 + t * 4 + s % 4


def split(x):
    high = x.astype(BF16)
    return high, (x - high.astype(F32)).astype(BF16)


def kernel(
    coherency,
    observed,
    flags_in,
    tile_map_in,
    jones_in,
    stage,
    owned,
    coh_raw,
    obs_raw,
    rows,
    obs_rows,
    coh,
    gains,
    m_all,
    n_all,
    partial,
    taken,
    residual,
    weight,
    val_p,
    val_q,
    pay,
    paid,
    jones_all,
    collect,
    spread,
    chosen_lane,
    flags,
    tile_map,
    jones,
    local_sem,
    send_sem,
    recv_sem,
    near_sem,
):
    tile, me = lax.axis_index("tile"), lax.axis_index("dir")
    y, z, core = tile // (Z * CORES), tile // CORES % Z, tile % CORES

    def at(dy, dz, dc):
        return (
            lax.rem(y + dy, YH) * (Z * CORES)
            + lax.rem(z + dz, Z) * CORES
            + lax.rem(core + dc, CORES)
        )

    def along_dir(dx, dl):
        return lax.rem(me // 2 + dx, DIRS // 2) * 2 + lax.rem(me + dl, 2)

    def remote(src, dst, send, recv, device):
        return pltpu.make_async_remote_copy(
            src_ref=src,
            dst_ref=dst,
            send_sem=send,
            recv_sem=recv,
            device_id=device,
            device_id_type=MESH,
        )

    barrier = pltpu.get_barrier_semaphore()
    greeted = (
        [(at(0, dz, 0), me) for dz in Z_FAR_FIRST]
        + [(at(dy, 0, dc), me) for dy, dc in YC_FAR_FIRST]
        + [(tile, along_dir(dx, dl)) for dx, dl in DIR_FAR_FIRST]
    )
    for device in greeted:
        pl.semaphore_signal(barrier, inc=1, device_id=device, device_id_type=MESH)

    here = [
        pltpu.make_async_copy(src, dst, local_sem.at[number])
        for number, (src, dst) in enumerate(
            (
                (jones_in, jones),
                (flags_in, flags),
                (tile_map_in, tile_map),
                (coherency, coh_raw),
                (observed, obs_raw),
            )
        )
    ]
    for copy in here:
        copy.start()

    here[0].wait()
    mine_at = lax.broadcasted_iota(jnp.int32, (8, 128), 1) // 8
    component = lax.broadcasted_iota(jnp.int32, (8, 128), 0)
    for pair in range(3):
        packed = jnp.zeros((8, 128), F32)
        for k in range(2):
            wide = jnp.concatenate([jones[2 * pair + k], jnp.zeros((8, 120), F32)], axis=1)
            for shift in (8, 16, 32):
                wide = wide + pltpu.roll(wide, shift, 1)
            wide = pltpu.roll(wide, 64, 1) if k else wide
            packed = jnp.where(mine_at == 8 * k + component, wide, packed)
        jones_all[tile, pair : pair + 1] = jnp.sum(packed, axis=0, keepdims=True)

    pl.semaphore_wait(barrier, len(greeted))

    mine = jones_all.at[tile]
    for dz in Z_FAR_FIRST:
        remote(mine, mine, send_sem.at[0], near_sem.at[dz], (at(0, dz, 0), me)).start()
    for dy, dc in YC_FAR_FIRST:
        remote(mine, mine, send_sem.at[0], recv_sem.at[0], (at(dy, 0, dc), me)).start()
    for copy in here[1:]:
        copy.wait()

    def to_rows(k, carry):
        for t in range(2):
            for s in range(12):
                block = coh_raw[t, k, s].astype(F32)
                for h in range(2):
                    rows[h, k, pl.ds(row_of(t, s) * 8, 8), :] = block[:, h * 128 : h * 128 + 128]
        for h in range(2):
            for c in range(8):
                coh[k, h, c] = rows[h, k, pl.ds(c, 24, stride=8), :].reshape(3, 8, 128)
        return carry

    lax.fori_loop(0, 6, to_rows, 0)
    for t in range(2):
        for s in range(12):
            block = obs_raw[t, s].astype(F32)
            for h in range(2):
                obs_rows[h, pl.ds(row_of(t, s) * 8, 8), :] = block[:, h * 128 : h * 128 + 128]

    second = lax.broadcasted_iota(jnp.int32, (8, 128), 0) >= 4
    for h in range(2):
        baseline = lax.broadcasted_iota(jnp.int32, (8, 128), 1) + 128 * h
        upper = jnp.where(baseline // SB < baseline % SB, 1, 0)
        for g in range(3):
            both = []
            for t in range(2):
                ahead = jnp.where(tile_map[t, 0] < tile_map[t, 1], 1, 0)
                kept = 1 - flags[t, g]
                both.append((jnp.maximum(upper, ahead) * kept).astype(F32))
            weight[h, g] = jnp.where(second, both[1], both[0])

    row = lax.broadcasted_iota(jnp.int32, (48, 256), 0)
    lane = lax.broadcasted_iota(jnp.int32, (48, 256), 1)
    chosen_lane[...] = jnp.where(lane % 128 // 8 == row % 16, 1.0, 0.0)
    station = lax.broadcasted_iota(jnp.int32, (256, 256), 0)
    station = station // 128 * 8 + station % 8
    baseline = lax.broadcasted_iota(jnp.int32, (256, 256), 1)
    for side in range(2):
        takes = station == (baseline % SB if side else baseline // SB)
        spread[side] = jnp.where(takes, 1.0, 0.0).astype(BF16)
    baseline = lax.broadcasted_iota(jnp.int32, (256, 256), 0)
    station = lax.broadcasted_iota(jnp.int32, (256, 256), 1)
    station = station // 128 * 8 + station % 8
    for side in range(2):
        own = station == (baseline % SB if side else baseline // SB)
        collect[side] = jnp.where(own, 1.0, 0.0).astype(BF16)
    val_p[15] = jnp.zeros((8, 256), F32)
    val_q[15] = jnp.zeros((8, 256), F32)

    for dz in Z_NEAR_FIRST:
        piece = jones_all.at[at(0, Z - dz, 0)]
        remote(piece, piece, send_sem.at[0], near_sem.at[dz], (at(0, dz, 0), me)).wait_recv()
        for dy, dc in YC_FAR_FIRST:
            remote(piece, piece, send_sem.at[0], recv_sem.at[0], (at(dy, 0, dc), me)).start()
    count = 7 * Z
    far = jones_all.at[pl.ds(0, count)]
    remote(far, far, send_sem.at[0], recv_sem.at[0], (at(1, 0, 0), me)).wait_recv()

    mask = chosen_lane[...]
    for side in range(2):
        picked = []
        for t in range(2):
            block = tile_map[t, side]
            both = jnp.concatenate([jones_all[2 * block], jones_all[2 * block + 1]], axis=1)
            rows_of = [jnp.broadcast_to(both[pair : pair + 1], (16, 256)) for pair in range(3)]
            picked.append(jnp.where(mask != 0.0, jnp.concatenate(rows_of, axis=0), 0.0))
        high, low = split(jnp.concatenate(picked, axis=0))
        full = jnp.dot(
            jnp.concatenate([high, low], axis=0), spread[side], preferred_element_type=F32
        )
        full = full[0:96] + full[96:192]
        for t in range(2):
            for h in range(2):
                block = full[t * 48 : t * 48 + 48, h * 128 : h * 128 + 128]
                gains[side, t, h] = block.reshape(6, 8, 128)

    def gain(side, k, h):
        return [
            jnp.where(
                second,
                jnp.broadcast_to(gains[side, 1, h, k, pl.ds(c, 1), :], (8, 128)),
                jnp.broadcast_to(gains[side, 0, h, k, pl.ds(c, 1), :], (8, 128)),
            )
            for c in range(8)
        ]

    for h in range(2):

        def add_direction(k, total, h=h):
            p, q = gain(0, k, h), gain(1, k, h)
            out = []
            for g in range(3):
                m = times_adjoint([coh[k, h, c, g] for c in range(8)], q)
                for c in range(8):
                    m_all[k, h, c, g] = m[c]
                v = times(p, m)
                out += [total[g * 8 + c] + v[c] for c in range(8)]
            return tuple(out)

        total = lax.fori_loop(0, 6, add_direction, (jnp.zeros((8, 128), F32),) * 24, unroll=2)
        for g in range(3):
            for c in range(8):
                partial[c, h, g] = total[g * 8 + c]

        for number, (dx, dl) in enumerate(DIR_FAR_FIRST):
            other = along_dir(dx, dl)
            remote(
                partial.at[other, h],
                taken.at[h, number],
                send_sem.at[1],
                recv_sem.at[1 + h],
                (tile, other),
            ).start()

    for h in range(2):

        def two_directions(pair, carry, h=h):
            rows_p, rows_q = [], []
            for j in range(2):
                k = pair * 2 + j
                p = gain(0, k, h)
                cp, cq = [0.0, 0.0], [0.0, 0.0]
                for g in range(3):
                    n = times(p, [coh[k, h, c, g] for c in range(8)])
                    for c in range(8):
                        n_all[k, h, c, g] = n[c]
                    m = [m_all[k, h, c, g] for c in range(8)]
                    w = weight[h, g]
                    for c in range(2):
                        cp[c] = cp[c] + w * sum(m[e] * m[e] for e in (2 * c, 2 * c + 1, 4 + 2 * c, 5 + 2 * c))
                        cq[c] = cq[c] + w * sum(n[e] * n[e] for e in (c, c + 2, c + 4, c + 6))
                rows_p += cp
                rows_q += cq
            val_p[12 + pair, :, h * 128 : h * 128 + 128] = fold(rows_p)
            val_q[12 + pair, :, h * 128 : h * 128 + 128] = fold(rows_q)
            return carry

        lax.fori_loop(0, 3, two_directions, 0)

    for h in range(2):
        got = taken.at[h]
        remote(got, got, send_sem.at[1], recv_sem.at[1 + h], (tile, me)).wait_recv()
        model = partial[me, h]
        for r in range(DIRS - 1):
            model = model + taken[h, r]
        seen = obs_rows[h, pl.ds(me, 24, stride=8), :].reshape(3, 8, 128)
        residual[h, me] = weight[h] * (seen - model)
        done = residual.at[h, me]
        for dx, dl in DIR_FAR_FIRST:
            other = along_dir(dx, dl)
            remote(done, done, send_sem.at[2], recv_sem.at[3 + h], (tile, other)).start()

    for h in range(2):
        got = residual.at[h, pl.ds(0, DIRS - 1)]
        remote(got, got, send_sem.at[2], recv_sem.at[3 + h], (tile, me)).wait_recv()

        def one_direction(k, carry, h=h):
            a, b = None, None
            for g in range(3):
                res = [residual[h, c, g] for c in range(8)]
                u = times_adjoint(res, [m_all[k, h, c, g] for c in range(8)])
                v = adjoint_times(res, [n_all[k, h, c, g] for c in range(8)])
                a = u if a is None else [i + j for i, j in zip(a, u)]
                b = v if b is None else [i + j for i, j in zip(b, v)]
            for j in range(2):
                val_p[2 * k + j, :, h * 128 : h * 128 + 128] = fold(a[4 * j : 4 * j + 4])
                val_q[2 * k + j, :, h * 128 : h * 128 + 128] = fold(b[4 * j : 4 * j + 4])
            return carry

        lax.fori_loop(0, 6, one_direction, 0)

    group = lax.broadcasted_iota(jnp.int32, (8, 128), 1) // 8
    parts = []
    for side, val in ((0, val_p), (1, val_q)):
        high, low = split(val[...].reshape(128, 256))
        sums = jnp.dot(
            jnp.concatenate([high, low], axis=0), collect[side], preferred_element_type=F32
        )
        sums = (sums[0:128] + sums[128:256]).reshape(16, 8, 256)
        halves = []
        for h in range(2):
            piece = jnp.zeros((8, 128), F32)
            for g in range(15):
                piece = jnp.where(group == g, sums[g, :, h * 128 : h * 128 + 128], piece)
            halves.append(piece)
        parts.append((side, 0, jnp.where(second, pltpu.roll(halves[1], 4, 0), halves[0])))
        parts.append((side, 1, jnp.where(second, halves[1], pltpu.roll(halves[0], 4, 0))))

    for b in range(TILES // 2):
        block = jnp.zeros((8, 128), F32)
        for side, t, part in parts:
            block = block + jnp.where(tile_map[t, side] == b, part, 0.0)
        pay[2 * b] = block[0:4]
        pay[2 * b + 1] = block[4:8]

    for number, (dy, dz, dc) in enumerate(FAR_FIRST):
        owner = at(dy, dz, dc)
        remote(
            pay.at[owner], paid.at[number], send_sem.at[3], recv_sem.at[5], (owner, me)
        ).start()

    half, part = me // 4, me % 4
    for c in range(8):
        wide = residual[half, c].reshape(24, 128)
        wide = pltpu.roll(wide, lax.rem(128 - 32 * part, 128), 1)
        stage[pl.ds(c, 24, stride=8), :] = wide

    remote(paid, paid, send_sem.at[3], recv_sem.at[5], (tile, me)).wait_recv()
    terms = [pay[tile]] + [paid[number] for number in range(TILES - 1)]
    while len(terms) > 1:
        terms = [a + b for a, b in zip(terms[::2], terms[1::2])]
    owned[...] = terms[0] * (1.0 / (12 * SB))

    sent = jones_all.at[pl.ds(0, TILES - 1)]
    remote(sent, sent, send_sem.at[0], recv_sem.at[0], (tile, me)).wait_send()
    remote(taken, taken, send_sem.at[1], recv_sem.at[1], (tile, me)).wait_send()
    remote(taken, taken, send_sem.at[2], recv_sem.at[1], (tile, me)).wait_send()
    remote(paid, paid, send_sem.at[3], recv_sem.at[5], (tile, me)).wait_send()


def unpack(stage, owned, res_out, grad_out, curv_out, res, grad, curv, sem):
    total = owned[...]
    moved = [(pltpu.roll(total, 128 - 8 * g, 1) if g else total)[:, 0:8] for g in range(15)]
    for k in range(6):
        grad[k] = jnp.concatenate(moved[2 * k : 2 * k + 2], axis=0)
        curv[k] = moved[12 + k // 2][k % 2 * 2 : k % 2 * 2 + 2]
    for t in range(2):
        for s in range(12):
            res[t, s] = stage[pl.ds(row_of(t, s) * 8, 8), 0:32]
    copies = [
        pltpu.make_async_copy(src, dst, sem.at[number])
        for number, (src, dst) in enumerate(((res, res_out), (grad, grad_out), (curv, curv_out)))
    ]
    for copy in copies:
        copy.start()
    for copy in copies:
        copy.wait()


def body(coherency, observed, flags, tile_map, jones):
    vmem, hbm = (pl.BlockSpec(memory_space=m) for m in (pltpu.VMEM, pltpu.HBM))
    scratch = [
        pltpu.VMEM((2, 6, 12, 8, 256), BF16),
        pltpu.VMEM((2, 12, 8, 256), BF16),
        pltpu.VMEM((2, 6, 192, 128), F32),
        pltpu.VMEM((2, 192, 128), F32),
        pltpu.VMEM((6, 2, 8, 3, 8, 128), F32),
        pltpu.VMEM((2, 2, 2, 6, 8, 128), F32),
        pltpu.VMEM((6, 2, 8, 3, 8, 128), F32),
        pltpu.VMEM((6, 2, 8, 3, 8, 128), F32),
        pltpu.VMEM((8, 2, 3, 8, 128), F32),
        pltpu.VMEM((2, 7, 3, 8, 128), F32),
        pltpu.VMEM((2, 8, 3, 8, 128), F32),
        pltpu.VMEM((2, 3, 8, 128), F32),
        pltpu.VMEM((16, 8, 256), F32),
        pltpu.VMEM((16, 8, 256), F32),
        pltpu.VMEM((TILES, 4, 128), F32),
        pltpu.VMEM((TILES - 1, 4, 128), F32),
        pltpu.VMEM((TILES, 3, 128), F32),
        pltpu.VMEM((2, 256, 256), BF16),
        pltpu.VMEM((2, 256, 256), BF16),
        pltpu.VMEM((48, 256), F32),
        pltpu.SMEM((2, 3), jnp.int32),
        pltpu.SMEM((2, 2), jnp.int32),
        pltpu.VMEM((6, 8, 8), F32),
        pltpu.SemaphoreType.DMA((5,)),
        pltpu.SemaphoreType.DMA((4,)),
        pltpu.SemaphoreType.DMA((6,)),
        pltpu.SemaphoreType.DMA((Z,)),
    ]
    summed = pl.pallas_call(
        kernel,
        out_shape=(
            jax.ShapeDtypeStruct((192, 128), F32),
            jax.ShapeDtypeStruct((4, 128), F32),
        ),
        in_specs=[hbm] * 5,
        out_specs=(vmem, vmem),
        scratch_shapes=scratch,
        compiler_params=pltpu.CompilerParams(
            collective_id=0, has_side_effects=True, vmem_limit_bytes=40 * 1024 * 1024
        ),
    )(*(pltpu.with_memory_space_constraint(x, pltpu.HBM) for x in (coherency, observed, flags, tile_map, jones)))
    shapes = ((2, 12, 8, 32), (6, 8, 8), (6, 2, 8))
    return pl.pallas_call(
        unpack,
        out_shape=tuple(jax.ShapeDtypeStruct(shape, F32) for shape in shapes),
        in_specs=[vmem, vmem],
        out_specs=(hbm, hbm, hbm),
        scratch_shapes=[pltpu.VMEM(shape, F32) for shape in shapes] + [pltpu.SemaphoreType.DMA((3,))],
        compiler_params=pltpu.CompilerParams(vmem_limit_bytes=8 * 1024 * 1024),
    )(*summed)


def solution(mesh):
    return jax.shard_map(
        body,
        mesh=mesh,
        in_specs=(
            P("tile", "dir", None, None, None),
            P("tile", None, None, None),
            P("tile", None),
            P("tile", None),
            P("dir", None, "tile"),
        ),
        out_specs=(P("tile", None, None, "dir"), P("dir", None, "tile"), P("dir", None, "tile")),
        check_vma=False,
    )
```

```python
import functools

import jax
import jax.numpy as jnp
from jax import lax
from jax.experimental import pallas as pl
from jax.experimental.pallas import tpu as pltpu
from jax.sharding import PartitionSpec as P

MESH = pl.DeviceIdType.MESH
YH, Z, CORES, DIRS = 4, 8, 2, 8
TILES = YH * Z * CORES
SB = 16
F32 = jnp.float32
BF16 = jnp.bfloat16


def hops(offset):
    y, z, c = offset
    return 2 * min(y, YH - y) + min(z, Z - z) + 0.5 * c


FAR_FIRST = sorted(
    (
        (y, z, c)
        for y in range(YH)
        for z in range(Z)
        for c in range(CORES)
        if (y, z, c) != (0, 0, 0)
    ),
    key=lambda o: -hops(o),
)
Z_NEAR_FIRST = (1, 7, 2, 6, 3, 5, 4)
Z_FAR_FIRST = (4, 3, 5, 2, 6, 1, 7)
DIR_FAR_FIRST = ((2, 1), (2, 0), (1, 1), (3, 1), (1, 0), (3, 0), (0, 1))
YC_FAR_FIRST = ((2, 1), (2, 0), (1, 1), (3, 1), (1, 0), (3, 0), (0, 1))


def times_adjoint(a, b):
    re, im = [], []
    for r in range(2):
        for c in range(2):
            x, y = None, None
            for m in range(2):
                ar, ai, br, bi = a[r * 2 + m], a[4 + r * 2 + m], b[c * 2 + m], b[4 + c * 2 + m]
                xr, xi = ar * br + ai * bi, ai * br - ar * bi
                x, y = (xr, xi) if x is None else (x + xr, y + xi)
            re.append(x)
            im.append(y)
    return re + im


def times(a, b):
    re, im = [], []
    for r in range(2):
        for c in range(2):
            x, y = None, None
            for m in range(2):
                ar, ai, br, bi = a[r * 2 + m], a[4 + r * 2 + m], b[m * 2 + c], b[4 + m * 2 + c]
                xr, xi = ar * br - ai * bi, ar * bi + ai * br
                x, y = (xr, xi) if x is None else (x + xr, y + xi)
            re.append(x)
            im.append(y)
    return re + im


def adjoint_times(a, b):
    re, im = [], []
    for r in range(2):
        for c in range(2):
            x, y = None, None
            for m in range(2):
                ar, ai, br, bi = a[m * 2 + r], a[4 + m * 2 + r], b[m * 2 + c], b[4 + m * 2 + c]
                xr, xi = ar * br + ai * bi, ar * bi - ai * br
                x, y = (xr, xi) if x is None else (x + xr, y + xi)
            re.append(x)
            im.append(y)
    return re + im


def fold(values):
    row = lax.broadcasted_iota(jnp.int32, (8, 128), 0)
    first, even = row % 4 < 2, row % 2 == 0
    a, b, c, d = values
    e = jnp.where(first, a, pltpu.roll(c, 2, 0)) + jnp.where(first, pltpu.roll(a, 6, 0), c)
    f = jnp.where(first, b, pltpu.roll(d, 2, 0)) + jnp.where(first, pltpu.roll(b, 6, 0), d)
    return jnp.where(even, e, pltpu.roll(f, 1, 0)) + jnp.where(even, pltpu.roll(e, 7, 0), f)


def row_of(t, s):
    return s // 4 * 8 + t * 4 + s % 4


def split(x):
    high = x.astype(BF16)
    return high, (x - high.astype(F32)).astype(BF16)


def kernel(
    coherency,
    observed,
    flags_in,
    tile_map_in,
    jones_in,
    stage,
    owned,
    coh_raw,
    obs_raw,
    rows,
    obs_rows,
    coh,
    gains,
    m_all,
    n_all,
    partial,
    taken,
    residual,
    weight,
    val_p,
    val_q,
    pay,
    paid,
    jones_all,
    collect,
    spread,
    chosen_lane,
    flags,
    tile_map,
    jones,
    local_sem,
    send_sem,
    recv_sem,
    near_sem,
):
    tile, me = lax.axis_index("tile"), lax.axis_index("dir")
    y, z, core = tile // (Z * CORES), tile // CORES % Z, tile % CORES

    def at(dy, dz, dc):
        return (
            lax.rem(y + dy, YH) * (Z * CORES)
            + lax.rem(z + dz, Z) * CORES
            + lax.rem(core + dc, CORES)
        )

    def along_dir(dx, dl):
        return lax.rem(me // 2 + dx, DIRS // 2) * 2 + lax.rem(me + dl, 2)

    def remote(src, dst, send, recv, device):
        return pltpu.make_async_remote_copy(
            src_ref=src,
            dst_ref=dst,
            send_sem=send,
            recv_sem=recv,
            device_id=device,
            device_id_type=MESH,
        )

    barrier = pltpu.get_barrier_semaphore()
    greeted = (
        [(at(0, dz, 0), me) for dz in Z_FAR_FIRST]
        + [(at(dy, 0, dc), me) for dy, dc in YC_FAR_FIRST]
        + [(tile, along_dir(dx, dl)) for dx, dl in DIR_FAR_FIRST]
    )
    for device in greeted:
        pl.semaphore_signal(barrier, inc=1, device_id=device, device_id_type=MESH)

    here = [
        pltpu.make_async_copy(src, dst, local_sem.at[number])
        for number, (src, dst) in enumerate(
            (
                (jones_in, jones),
                (flags_in, flags),
                (tile_map_in, tile_map),
                (coherency, coh_raw),
                (observed, obs_raw),
            )
        )
    ]
    for copy in here:
        copy.start()

    here[0].wait()
    mine_at = lax.broadcasted_iota(jnp.int32, (8, 128), 1) // 8
    component = lax.broadcasted_iota(jnp.int32, (8, 128), 0)
    for pair in range(3):
        packed = jnp.zeros((8, 128), F32)
        for k in range(2):
            wide = jnp.concatenate([jones[2 * pair + k], jnp.zeros((8, 120), F32)], axis=1)
            for shift in (8, 16, 32):
                wide = wide + pltpu.roll(wide, shift, 1)
            wide = pltpu.roll(wide, 64, 1) if k else wide
            packed = jnp.where(mine_at == 8 * k + component, wide, packed)
        jones_all[tile, pair : pair + 1] = jnp.sum(packed, axis=0, keepdims=True)

    pl.semaphore_wait(barrier, len(greeted))

    mine = jones_all.at[tile]
    for dz in Z_FAR_FIRST:
        remote(mine, mine, send_sem.at[0], near_sem.at[dz], (at(0, dz, 0), me)).start()
    for dy, dc in YC_FAR_FIRST:
        remote(mine, mine, send_sem.at[0], recv_sem.at[0], (at(dy, 0, dc), me)).start()
    for copy in here[1:]:
        copy.wait()

    def to_rows(k, carry):
        for t in range(2):
            for s in range(12):
                block = coh_raw[t, k, s].astype(F32)
                for h in range(2):
                    rows[h, k, pl.ds(row_of(t, s) * 8, 8), :] = block[:, h * 128 : h * 128 + 128]
        for h in range(2):
            for c in range(8):
                coh[k, h, c] = rows[h, k, pl.ds(c, 24, stride=8), :].reshape(3, 8, 128)
        return carry

    lax.fori_loop(0, 6, to_rows, 0)
    for t in range(2):
        for s in range(12):
            block = obs_raw[t, s].astype(F32)
            for h in range(2):
                obs_rows[h, pl.ds(row_of(t, s) * 8, 8), :] = block[:, h * 128 : h * 128 + 128]

    second = lax.broadcasted_iota(jnp.int32, (8, 128), 0) >= 4
    for h in range(2):
        baseline = lax.broadcasted_iota(jnp.int32, (8, 128), 1) + 128 * h
        upper = jnp.where(baseline // SB < baseline % SB, 1, 0)
        for g in range(3):
            both = []
            for t in range(2):
                ahead = jnp.where(tile_map[t, 0] < tile_map[t, 1], 1, 0)
                kept = 1 - flags[t, g]
                both.append((jnp.maximum(upper, ahead) * kept).astype(F32))
            weight[h, g] = jnp.where(second, both[1], both[0])

    row = lax.broadcasted_iota(jnp.int32, (48, 256), 0)
    lane = lax.broadcasted_iota(jnp.int32, (48, 256), 1)
    chosen_lane[...] = jnp.where(lane % 128 // 8 == row % 16, 1.0, 0.0)
    station = lax.broadcasted_iota(jnp.int32, (256, 256), 0)
    station = station // 128 * 8 + station % 8
    baseline = lax.broadcasted_iota(jnp.int32, (256, 256), 1)
    for side in range(2):
        takes = station == (baseline % SB if side else baseline // SB)
        spread[side] = jnp.where(takes, 1.0, 0.0).astype(BF16)
    baseline = lax.broadcasted_iota(jnp.int32, (256, 256), 0)
    station = lax.broadcasted_iota(jnp.int32, (256, 256), 1)
    station = station // 128 * 8 + station % 8
    for side in range(2):
        own = station == (baseline % SB if side else baseline // SB)
        collect[side] = jnp.where(own, 1.0, 0.0).astype(BF16)
    val_p[15] = jnp.zeros((8, 256), F32)
    val_q[15] = jnp.zeros((8, 256), F32)

    for dz in Z_NEAR_FIRST:
        piece = jones_all.at[at(0, Z - dz, 0)]
        remote(piece, piece, send_sem.at[0], near_sem.at[dz], (at(0, dz, 0), me)).wait_recv()
        for dy, dc in YC_FAR_FIRST:
            remote(piece, piece, send_sem.at[0], recv_sem.at[0], (at(dy, 0, dc), me)).start()
    count = 7 * Z
    far = jones_all.at[pl.ds(0, count)]
    remote(far, far, send_sem.at[0], recv_sem.at[0], (at(1, 0, 0), me)).wait_recv()

    mask = chosen_lane[...]
    for side in range(2):
        picked = []
        for t in range(2):
            block = tile_map[t, side]
            both = jnp.concatenate([jones_all[2 * block], jones_all[2 * block + 1]], axis=1)
            rows_of = [jnp.broadcast_to(both[pair : pair + 1], (16, 256)) for pair in range(3)]
            picked.append(jnp.where(mask != 0.0, jnp.concatenate(rows_of, axis=0), 0.0))
        high, low = split(jnp.concatenate(picked, axis=0))
        full = jnp.dot(
            jnp.concatenate([high, low], axis=0), spread[side], preferred_element_type=F32
        )
        full = full[0:96] + full[96:192]
        for t in range(2):
            for h in range(2):
                block = full[t * 48 : t * 48 + 48, h * 128 : h * 128 + 128]
                gains[side, t, h] = block.reshape(6, 8, 128)

    def gain(side, k, h):
        return [
            jnp.where(
                second,
                jnp.broadcast_to(gains[side, 1, h, k, pl.ds(c, 1), :], (8, 128)),
                jnp.broadcast_to(gains[side, 0, h, k, pl.ds(c, 1), :], (8, 128)),
            )
            for c in range(8)
        ]

    for h in range(2):

        def add_direction(k, total, h=h):
            p, q = gain(0, k, h), gain(1, k, h)
            out = []
            for g in range(3):
                m = times_adjoint([coh[k, h, c, g] for c in range(8)], q)
                for c in range(8):
                    m_all[k, h, c, g] = m[c]
                v = times(p, m)
                out += [total[g * 8 + c] + v[c] for c in range(8)]
            return tuple(out)

        total = lax.fori_loop(0, 6, add_direction, (jnp.zeros((8, 128), F32),) * 24, unroll=2)
        for g in range(3):
            for c in range(8):
                partial[c, h, g] = total[g * 8 + c]

        for number, (dx, dl) in enumerate(DIR_FAR_FIRST):
            other = along_dir(dx, dl)
            remote(
                partial.at[other, h],
                taken.at[h, number],
                send_sem.at[1],
                recv_sem.at[1 + h],
                (tile, other),
            ).start()

    for h in range(2):

        def two_directions(pair, carry, h=h):
            rows_p, rows_q = [], []
            for j in range(2):
                k = pair * 2 + j
                p = gain(0, k, h)
                cp, cq = [0.0, 0.0], [0.0, 0.0]
                for g in range(3):
                    n = times(p, [coh[k, h, c, g] for c in range(8)])
                    for c in range(8):
                        n_all[k, h, c, g] = n[c]
                    m = [m_all[k, h, c, g] for c in range(8)]
                    w = weight[h, g]
                    for c in range(2):
                        cp[c] = cp[c] + w * sum(m[e] * m[e] for e in (2 * c, 2 * c + 1, 4 + 2 * c, 5 + 2 * c))
                        cq[c] = cq[c] + w * sum(n[e] * n[e] for e in (c, c + 2, c + 4, c + 6))
                rows_p += cp
                rows_q += cq
            val_p[12 + pair, :, h * 128 : h * 128 + 128] = fold(rows_p)
            val_q[12 + pair, :, h * 128 : h * 128 + 128] = fold(rows_q)
            return carry

        lax.fori_loop(0, 3, two_directions, 0)

    for h in range(2):
        got = taken.at[h]
        remote(got, got, send_sem.at[1], recv_sem.at[1 + h], (tile, me)).wait_recv()
        model = partial[me, h]
        for r in range(DIRS - 1):
            model = model + taken[h, r]
        seen = obs_rows[h, pl.ds(me, 24, stride=8), :].reshape(3, 8, 128)
        residual[h, me] = weight[h] * (seen - model)
        done = residual.at[h, me]
        for dx, dl in DIR_FAR_FIRST:
            other = along_dir(dx, dl)
            remote(done, done, send_sem.at[2], recv_sem.at[3 + h], (tile, other)).start()

    for h in range(2):
        got = residual.at[h, pl.ds(0, DIRS - 1)]
        remote(got, got, send_sem.at[2], recv_sem.at[3 + h], (tile, me)).wait_recv()

        def one_direction(k, carry, h=h):
            a, b = None, None
            for g in range(3):
                res = [residual[h, c, g] for c in range(8)]
                u = times_adjoint(res, [m_all[k, h, c, g] for c in range(8)])
                v = adjoint_times(res, [n_all[k, h, c, g] for c in range(8)])
                a = u if a is None else [i + j for i, j in zip(a, u)]
                b = v if b is None else [i + j for i, j in zip(b, v)]
            for j in range(2):
                val_p[2 * k + j, :, h * 128 : h * 128 + 128] = fold(a[4 * j : 4 * j + 4])
                val_q[2 * k + j, :, h * 128 : h * 128 + 128] = fold(b[4 * j : 4 * j + 4])
            return carry

        lax.fori_loop(0, 6, one_direction, 0, unroll=3)

    group = lax.broadcasted_iota(jnp.int32, (8, 128), 1) // 8
    parts = []
    for side, val in ((0, val_p), (1, val_q)):
        high, low = split(val[...].reshape(128, 256))
        sums = jnp.dot(
            jnp.concatenate([high, low], axis=0), collect[side], preferred_element_type=F32
        )
        sums = (sums[0:128] + sums[128:256]).reshape(16, 8, 256)
        halves = []
        for h in range(2):
            piece = jnp.zeros((8, 128), F32)
            for g in range(15):
                piece = jnp.where(group == g, sums[g, :, h * 128 : h * 128 + 128], piece)
            halves.append(piece)
        parts.append((side, 0, jnp.where(second, pltpu.roll(halves[1], 4, 0), halves[0])))
        parts.append((side, 1, jnp.where(second, halves[1], pltpu.roll(halves[0], 4, 0))))

    for b in range(TILES // 2):
        block = jnp.zeros((8, 128), F32)
        for side, t, part in parts:
            block = block + jnp.where(tile_map[t, side] == b, part, 0.0)
        pay[2 * b] = block[0:4]
        pay[2 * b + 1] = block[4:8]

    for number, (dy, dz, dc) in enumerate(FAR_FIRST):
        owner = at(dy, dz, dc)
        remote(
            pay.at[owner], paid.at[number], send_sem.at[3], recv_sem.at[5], (owner, me)
        ).start()

    half, part = me // 4, me % 4
    for c in range(8):
        wide = residual[half, c].reshape(24, 128)
        wide = pltpu.roll(wide, lax.rem(128 - 32 * part, 128), 1)
        stage[pl.ds(c, 24, stride=8), :] = wide

    remote(paid, paid, send_sem.at[3], recv_sem.at[5], (tile, me)).wait_recv()
    terms = [pay[tile]] + [paid[number] for number in range(TILES - 1)]
    while len(terms) > 1:
        terms = [a + b for a, b in zip(terms[::2], terms[1::2])]
    owned[...] = terms[0] * (1.0 / (12 * SB))

    sent = jones_all.at[pl.ds(0, TILES - 1)]
    remote(sent, sent, send_sem.at[0], recv_sem.at[0], (tile, me)).wait_send()
    remote(taken, taken, send_sem.at[1], recv_sem.at[1], (tile, me)).wait_send()
    remote(taken, taken, send_sem.at[2], recv_sem.at[1], (tile, me)).wait_send()
    remote(paid, paid, send_sem.at[3], recv_sem.at[5], (tile, me)).wait_send()


def unpack(stage, owned, res_out, grad_out, curv_out, res, grad, curv, sem):
    total = owned[...]
    moved = [(pltpu.roll(total, 128 - 8 * g, 1) if g else total)[:, 0:8] for g in range(15)]
    for k in range(6):
        grad[k] = jnp.concatenate(moved[2 * k : 2 * k + 2], axis=0)
        curv[k] = moved[12 + k // 2][k % 2 * 2 : k % 2 * 2 + 2]
    for t in range(2):
        for s in range(12):
            res[t, s] = stage[pl.ds(row_of(t, s) * 8, 8), 0:32]
    copies = [
        pltpu.make_async_copy(src, dst, sem.at[number])
        for number, (src, dst) in enumerate(((res, res_out), (grad, grad_out), (curv, curv_out)))
    ]
    for copy in copies:
        copy.start()
    for copy in copies:
        copy.wait()


def body(coherency, observed, flags, tile_map, jones):
    vmem, hbm = (pl.BlockSpec(memory_space=m) for m in (pltpu.VMEM, pltpu.HBM))
    scratch = [
        pltpu.VMEM((2, 6, 12, 8, 256), BF16),
        pltpu.VMEM((2, 12, 8, 256), BF16),
        pltpu.VMEM((2, 6, 192, 128), F32),
        pltpu.VMEM((2, 192, 128), F32),
        pltpu.VMEM((6, 2, 8, 3, 8, 128), F32),
        pltpu.VMEM((2, 2, 2, 6, 8, 128), F32),
        pltpu.VMEM((6, 2, 8, 3, 8, 128), F32),
        pltpu.VMEM((6, 2, 8, 3, 8, 128), F32),
        pltpu.VMEM((8, 2, 3, 8, 128), F32),
        pltpu.VMEM((2, 7, 3, 8, 128), F32),
        pltpu.VMEM((2, 8, 3, 8, 128), F32),
        pltpu.VMEM((2, 3, 8, 128), F32),
        pltpu.VMEM((16, 8, 256), F32),
        pltpu.VMEM((16, 8, 256), F32),
        pltpu.VMEM((TILES, 4, 128), F32),
        pltpu.VMEM((TILES - 1, 4, 128), F32),
        pltpu.VMEM((TILES, 3, 128), F32),
        pltpu.VMEM((2, 256, 256), BF16),
        pltpu.VMEM((2, 256, 256), BF16),
        pltpu.VMEM((48, 256), F32),
        pltpu.SMEM((2, 3), jnp.int32),
        pltpu.SMEM((2, 2), jnp.int32),
        pltpu.VMEM((6, 8, 8), F32),
        pltpu.SemaphoreType.DMA((5,)),
        pltpu.SemaphoreType.DMA((4,)),
        pltpu.SemaphoreType.DMA((6,)),
        pltpu.SemaphoreType.DMA((Z,)),
    ]
    summed = pl.pallas_call(
        kernel,
        out_shape=(
            jax.ShapeDtypeStruct((192, 128), F32),
            jax.ShapeDtypeStruct((4, 128), F32),
        ),
        in_specs=[hbm] * 5,
        out_specs=(vmem, vmem),
        scratch_shapes=scratch,
        compiler_params=pltpu.CompilerParams(
            collective_id=0, has_side_effects=True, vmem_limit_bytes=40 * 1024 * 1024
        ),
    )(*(pltpu.with_memory_space_constraint(x, pltpu.HBM) for x in (coherency, observed, flags, tile_map, jones)))
    shapes = ((2, 12, 8, 32), (6, 8, 8), (6, 2, 8))
    return pl.pallas_call(
        unpack,
        out_shape=tuple(jax.ShapeDtypeStruct(shape, F32) for shape in shapes),
        in_specs=[vmem, vmem],
        out_specs=(hbm, hbm, hbm),
        scratch_shapes=[pltpu.VMEM(shape, F32) for shape in shapes] + [pltpu.SemaphoreType.DMA((3,))],
        compiler_params=pltpu.CompilerParams(vmem_limit_bytes=8 * 1024 * 1024),
    )(*summed)


def solution(mesh):
    return jax.shard_map(
        body,
        mesh=mesh,
        in_specs=(
            P("tile", "dir", None, None, None),
            P("tile", None, None, None),
            P("tile", None),
            P("tile", None),
            P("dir", None, "tile"),
        ),
        out_specs=(P("tile", None, None, "dir"), P("dir", None, "tile"), P("dir", None, "tile")),
        check_vma=False,
    )
```

```python
import functools

import jax
import jax.numpy as jnp
from jax import lax
from jax.experimental import pallas as pl
from jax.experimental.pallas import tpu as pltpu
from jax.sharding import PartitionSpec as P

MESH = pl.DeviceIdType.MESH
YH, Z, CORES, DIRS = 4, 8, 2, 8
TILES = YH * Z * CORES
SB = 16
F32 = jnp.float32
BF16 = jnp.bfloat16


def hops(offset):
    y, z, c = offset
    return 2 * min(y, YH - y) + min(z, Z - z) + 0.5 * c


FAR_FIRST = sorted(
    (
        (y, z, c)
        for y in range(YH)
        for z in range(Z)
        for c in range(CORES)
        if (y, z, c) != (0, 0, 0)
    ),
    key=lambda o: -hops(o),
)
Z_NEAR_FIRST = (1, 7, 2, 6, 3, 5, 4)
Z_FAR_FIRST = (4, 3, 5, 2, 6, 1, 7)
DIR_FAR_FIRST = ((2, 1), (2, 0), (1, 1), (3, 1), (1, 0), (3, 0), (0, 1))
YC_FAR_FIRST = ((2, 1), (2, 0), (1, 1), (3, 1), (1, 0), (3, 0), (0, 1))


def times_adjoint(a, b):
    re, im = [], []
    for r in range(2):
        for c in range(2):
            x, y = None, None
            for m in range(2):
                ar, ai, br, bi = a[r * 2 + m], a[4 + r * 2 + m], b[c * 2 + m], b[4 + c * 2 + m]
                xr, xi = ar * br + ai * bi, ai * br - ar * bi
                x, y = (xr, xi) if x is None else (x + xr, y + xi)
            re.append(x)
            im.append(y)
    return re + im


def times(a, b):
    re, im = [], []
    for r in range(2):
        for c in range(2):
            x, y = None, None
            for m in range(2):
                ar, ai, br, bi = a[r * 2 + m], a[4 + r * 2 + m], b[m * 2 + c], b[4 + m * 2 + c]
                xr, xi = ar * br - ai * bi, ar * bi + ai * br
                x, y = (xr, xi) if x is None else (x + xr, y + xi)
            re.append(x)
            im.append(y)
    return re + im


def adjoint_times(a, b):
    re, im = [], []
    for r in range(2):
        for c in range(2):
            x, y = None, None
            for m in range(2):
                ar, ai, br, bi = a[m * 2 + r], a[4 + m * 2 + r], b[m * 2 + c], b[4 + m * 2 + c]
                xr, xi = ar * br + ai * bi, ar * bi - ai * br
                x, y = (xr, xi) if x is None else (x + xr, y + xi)
            re.append(x)
            im.append(y)
    return re + im


def fold(values):
    row = lax.broadcasted_iota(jnp.int32, (8, 128), 0)
    first, even = row % 4 < 2, row % 2 == 0
    a, b, c, d = values
    e = jnp.where(first, a, pltpu.roll(c, 2, 0)) + jnp.where(first, pltpu.roll(a, 6, 0), c)
    f = jnp.where(first, b, pltpu.roll(d, 2, 0)) + jnp.where(first, pltpu.roll(b, 6, 0), d)
    return jnp.where(even, e, pltpu.roll(f, 1, 0)) + jnp.where(even, pltpu.roll(e, 7, 0), f)


def row_of(t, s):
    return s // 4 * 8 + t * 4 + s % 4


def split(x):
    high = x.astype(BF16)
    return high, (x - high.astype(F32)).astype(BF16)


def kernel(
    coherency,
    observed,
    flags_in,
    tile_map_in,
    jones_in,
    stage,
    owned,
    coh_raw,
    obs_raw,
    rows,
    obs_rows,
    coh,
    gains,
    m_all,
    n_all,
    partial,
    taken,
    residual,
    weight,
    val_p,
    val_q,
    pay,
    paid,
    jones_all,
    collect,
    spread,
    chosen_lane,
    flags,
    tile_map,
    jones,
    local_sem,
    send_sem,
    recv_sem,
    near_sem,
):
    tile, me = lax.axis_index("tile"), lax.axis_index("dir")
    y, z, core = tile // (Z * CORES), tile // CORES % Z, tile % CORES

    def at(dy, dz, dc):
        return (
            lax.rem(y + dy, YH) * (Z * CORES)
            + lax.rem(z + dz, Z) * CORES
            + lax.rem(core + dc, CORES)
        )

    def along_dir(dx, dl):
        return lax.rem(me // 2 + dx, DIRS // 2) * 2 + lax.rem(me + dl, 2)

    def remote(src, dst, send, recv, device):
        return pltpu.make_async_remote_copy(
            src_ref=src,
            dst_ref=dst,
            send_sem=send,
            recv_sem=recv,
            device_id=device,
            device_id_type=MESH,
        )

    barrier = pltpu.get_barrier_semaphore()
    greeted = (
        [(at(0, dz, 0), me) for dz in Z_FAR_FIRST]
        + [(at(dy, 0, dc), me) for dy, dc in YC_FAR_FIRST]
        + [(tile, along_dir(dx, dl)) for dx, dl in DIR_FAR_FIRST]
    )
    for device in greeted:
        pl.semaphore_signal(barrier, inc=1, device_id=device, device_id_type=MESH)

    here = [
        pltpu.make_async_copy(src, dst, local_sem.at[number])
        for number, (src, dst) in enumerate(
            (
                (jones_in, jones),
                (flags_in, flags),
                (tile_map_in, tile_map),
                (coherency, coh_raw),
                (observed, obs_raw),
            )
        )
    ]
    for copy in here:
        copy.start()

    here[0].wait()
    mine_at = lax.broadcasted_iota(jnp.int32, (8, 128), 1) // 8
    component = lax.broadcasted_iota(jnp.int32, (8, 128), 0)
    for pair in range(3):
        packed = jnp.zeros((8, 128), F32)
        for k in range(2):
            wide = jnp.concatenate([jones[2 * pair + k], jnp.zeros((8, 120), F32)], axis=1)
            for shift in (8, 16, 32):
                wide = wide + pltpu.roll(wide, shift, 1)
            wide = pltpu.roll(wide, 64, 1) if k else wide
            packed = jnp.where(mine_at == 8 * k + component, wide, packed)
        jones_all[tile, pair : pair + 1] = jnp.sum(packed, axis=0, keepdims=True)

    pl.semaphore_wait(barrier, len(greeted))

    mine = jones_all.at[tile]
    for dz in Z_FAR_FIRST:
        remote(mine, mine, send_sem.at[0], near_sem.at[dz], (at(0, dz, 0), me)).start()
    for dy, dc in YC_FAR_FIRST:
        remote(mine, mine, send_sem.at[0], recv_sem.at[0], (at(dy, 0, dc), me)).start()
    for copy in here[1:]:
        copy.wait()

    def to_rows(k, carry):
        for t in range(2):
            for s in range(12):
                block = coh_raw[t, k, s].astype(F32)
                for h in range(2):
                    rows[h, k, pl.ds(row_of(t, s) * 8, 8), :] = block[:, h * 128 : h * 128 + 128]
        for h in range(2):
            for c in range(8):
                coh[k, h, c] = rows[h, k, pl.ds(c, 24, stride=8), :].reshape(3, 8, 128)
        return carry

    lax.fori_loop(0, 6, to_rows, 0)
    for t in range(2):
        for s in range(12):
            block = obs_raw[t, s].astype(F32)
            for h in range(2):
                obs_rows[h, pl.ds(row_of(t, s) * 8, 8), :] = block[:, h * 128 : h * 128 + 128]

    second = lax.broadcasted_iota(jnp.int32, (8, 128), 0) >= 4
    for h in range(2):
        baseline = lax.broadcasted_iota(jnp.int32, (8, 128), 1) + 128 * h
        upper = jnp.where(baseline // SB < baseline % SB, 1, 0)
        for g in range(3):
            both = []
            for t in range(2):
                ahead = jnp.where(tile_map[t, 0] < tile_map[t, 1], 1, 0)
                kept = 1 - flags[t, g]
                both.append((jnp.maximum(upper, ahead) * kept).astype(F32))
            weight[h, g] = jnp.where(second, both[1], both[0])

    row = lax.broadcasted_iota(jnp.int32, (48, 256), 0)
    lane = lax.broadcasted_iota(jnp.int32, (48, 256), 1)
    chosen_lane[...] = jnp.where(lane % 128 // 8 == row % 16, 1.0, 0.0)
    station = lax.broadcasted_iota(jnp.int32, (256, 256), 0)
    station = station // 128 * 8 + station % 8
    baseline = lax.broadcasted_iota(jnp.int32, (256, 256), 1)
    for side in range(2):
        takes = station == (baseline % SB if side else baseline // SB)
        spread[side] = jnp.where(takes, 1.0, 0.0).astype(BF16)
    baseline = lax.broadcasted_iota(jnp.int32, (256, 256), 0)
    station = lax.broadcasted_iota(jnp.int32, (256, 256), 1)
    station = station // 128 * 8 + station % 8
    for side in range(2):
        own = station == (baseline % SB if side else baseline // SB)
        collect[side] = jnp.where(own, 1.0, 0.0).astype(BF16)
    val_p[15] = jnp.zeros((8, 256), F32)
    val_q[15] = jnp.zeros((8, 256), F32)

    for dz in Z_NEAR_FIRST:
        piece = jones_all.at[at(0, Z - dz, 0)]
        remote(piece, piece, send_sem.at[0], near_sem.at[dz], (at(0, dz, 0), me)).wait_recv()
        for dy, dc in YC_FAR_FIRST:
            remote(piece, piece, send_sem.at[0], recv_sem.at[0], (at(dy, 0, dc), me)).start()
    count = 7 * Z
    far = jones_all.at[pl.ds(0, count)]
    remote(far, far, send_sem.at[0], recv_sem.at[0], (at(1, 0, 0), me)).wait_recv()

    mask = chosen_lane[...]
    for side in range(2):
        picked = []
        for t in range(2):
            block = tile_map[t, side]
            both = jnp.concatenate([jones_all[2 * block], jones_all[2 * block + 1]], axis=1)
            rows_of = [jnp.broadcast_to(both[pair : pair + 1], (16, 256)) for pair in range(3)]
            picked.append(jnp.where(mask != 0.0, jnp.concatenate(rows_of, axis=0), 0.0))
        high, low = split(jnp.concatenate(picked, axis=0))
        full = jnp.dot(
            jnp.concatenate([high, low], axis=0), spread[side], preferred_element_type=F32
        )
        full = full[0:96] + full[96:192]
        for t in range(2):
            for h in range(2):
                block = full[t * 48 : t * 48 + 48, h * 128 : h * 128 + 128]
                gains[side, t, h] = block.reshape(6, 8, 128)

    def gain(side, k, h):
        return [
            jnp.where(
                second,
                jnp.broadcast_to(gains[side, 1, h, k, pl.ds(c, 1), :], (8, 128)),
                jnp.broadcast_to(gains[side, 0, h, k, pl.ds(c, 1), :], (8, 128)),
            )
            for c in range(8)
        ]

    for h in range(2):

        def add_direction(k, total, h=h):
            p, q = gain(0, k, h), gain(1, k, h)
            out = []
            for g in range(3):
                m = times_adjoint([coh[k, h, c, g] for c in range(8)], q)
                for c in range(8):
                    m_all[k, h, c, g] = m[c]
                v = times(p, m)
                out += [total[g * 8 + c] + v[c] for c in range(8)]
            return tuple(out)

        total = lax.fori_loop(0, 6, add_direction, (jnp.zeros((8, 128), F32),) * 24, unroll=2)
        for g in range(3):
            for c in range(8):
                partial[c, h, g] = total[g * 8 + c]

        for number, (dx, dl) in enumerate(DIR_FAR_FIRST):
            other = along_dir(dx, dl)
            remote(
                partial.at[other, h],
                taken.at[h, number],
                send_sem.at[1],
                recv_sem.at[1 + h],
                (tile, other),
            ).start()

    for h in range(2):

        def two_directions(pair, carry, h=h):
            rows_p, rows_q = [], []
            for j in range(2):
                k = pair * 2 + j
                p = gain(0, k, h)
                cp, cq = [0.0, 0.0], [0.0, 0.0]
                for g in range(3):
                    n = times(p, [coh[k, h, c, g] for c in range(8)])
                    for c in range(8):
                        n_all[k, h, c, g] = n[c]
                    m = [m_all[k, h, c, g] for c in range(8)]
                    w = weight[h, g]
                    for c in range(2):
                        cp[c] = cp[c] + w * sum(m[e] * m[e] for e in (2 * c, 2 * c + 1, 4 + 2 * c, 5 + 2 * c))
                        cq[c] = cq[c] + w * sum(n[e] * n[e] for e in (c, c + 2, c + 4, c + 6))
                rows_p += cp
                rows_q += cq
            val_p[12 + pair, :, h * 128 : h * 128 + 128] = fold(rows_p)
            val_q[12 + pair, :, h * 128 : h * 128 + 128] = fold(rows_q)
            return carry

        lax.fori_loop(0, 3, two_directions, 0)

    for h in range(2):
        got = taken.at[h]
        remote(got, got, send_sem.at[1], recv_sem.at[1 + h], (tile, me)).wait_recv()
        model = partial[me, h]
        for r in range(DIRS - 1):
            model = model + taken[h, r]
        seen = obs_rows[h, pl.ds(me, 24, stride=8), :].reshape(3, 8, 128)
        residual[h, me] = weight[h] * (seen - model)
        done = residual.at[h, me]
        for dx, dl in DIR_FAR_FIRST:
            other = along_dir(dx, dl)
            remote(done, done, send_sem.at[2], recv_sem.at[3 + h], (tile, other)).start()

    for h in range(2):
        got = residual.at[h, pl.ds(0, DIRS - 1)]
        remote(got, got, send_sem.at[2], recv_sem.at[3 + h], (tile, me)).wait_recv()

        def one_direction(k, carry, h=h):
            a, b = None, None
            for g in range(3):
                res = [residual[h, c, g] for c in range(8)]
                u = times_adjoint(res, [m_all[k, h, c, g] for c in range(8)])
                v = adjoint_times(res, [n_all[k, h, c, g] for c in range(8)])
                a = u if a is None else [i + j for i, j in zip(a, u)]
                b = v if b is None else [i + j for i, j in zip(b, v)]
            for j in range(2):
                val_p[2 * k + j, :, h * 128 : h * 128 + 128] = fold(a[4 * j : 4 * j + 4])
                val_q[2 * k + j, :, h * 128 : h * 128 + 128] = fold(b[4 * j : 4 * j + 4])
            return carry

        lax.fori_loop(0, 6, one_direction, 0)

    group = lax.broadcasted_iota(jnp.int32, (8, 128), 1) // 8
    parts = []
    for side, val in ((0, val_p), (1, val_q)):
        high, low = split(val[...].reshape(128, 256))
        sums = jnp.dot(
            jnp.concatenate([high, low], axis=0), collect[side], preferred_element_type=F32
        )
        sums = (sums[0:128] + sums[128:256]).reshape(16, 8, 256)
        halves = []
        for h in range(2):
            piece = jnp.zeros((8, 128), F32)
            for g in range(15):
                piece = jnp.where(group == g, sums[g, :, h * 128 : h * 128 + 128], piece)
            halves.append(piece)
        parts.append((side, 0, jnp.where(second, pltpu.roll(halves[1], 4, 0), halves[0])))
        parts.append((side, 1, jnp.where(second, halves[1], pltpu.roll(halves[0], 4, 0))))

    number = 0
    for dy, dz in dict.fromkeys(offset[:2] for offset in FAR_FIRST):
        b = lax.rem(y + dy, YH) * Z + lax.rem(z + dz, Z)
        block = jnp.zeros((8, 128), F32)
        for side, t, part in parts:
            block = block + jnp.where(tile_map[t, side] == b, part, 0.0)
        pay[2 * b] = block[0:4]
        pay[2 * b + 1] = block[4:8]
        for dc in (1, 0) if dy or dz else (1,):
            owner = at(dy, dz, dc)
            remote(
                pay.at[owner], paid.at[number], send_sem.at[3], recv_sem.at[5], (owner, me)
            ).start()
            number += 1

    half, part = me // 4, me % 4
    for c in range(8):
        wide = residual[half, c].reshape(24, 128)
        wide = pltpu.roll(wide, lax.rem(128 - 32 * part, 128), 1)
        stage[pl.ds(c, 24, stride=8), :] = wide

    remote(paid, paid, send_sem.at[3], recv_sem.at[5], (tile, me)).wait_recv()
    terms = [pay[tile]] + [paid[number] for number in range(TILES - 1)]
    while len(terms) > 1:
        terms = [a + b for a, b in zip(terms[::2], terms[1::2])]
    owned[...] = terms[0] * (1.0 / (12 * SB))

    sent = jones_all.at[pl.ds(0, TILES - 1)]
    remote(sent, sent, send_sem.at[0], recv_sem.at[0], (tile, me)).wait_send()
    remote(taken, taken, send_sem.at[1], recv_sem.at[1], (tile, me)).wait_send()
    remote(taken, taken, send_sem.at[2], recv_sem.at[1], (tile, me)).wait_send()
    remote(paid, paid, send_sem.at[3], recv_sem.at[5], (tile, me)).wait_send()


def unpack(stage, owned, res_out, grad_out, curv_out, res, grad, curv, sem):
    total = owned[...]
    moved = [(pltpu.roll(total, 128 - 8 * g, 1) if g else total)[:, 0:8] for g in range(15)]
    for k in range(6):
        grad[k] = jnp.concatenate(moved[2 * k : 2 * k + 2], axis=0)
        curv[k] = moved[12 + k // 2][k % 2 * 2 : k % 2 * 2 + 2]
    for t in range(2):
        for s in range(12):
            res[t, s] = stage[pl.ds(row_of(t, s) * 8, 8), 0:32]
    copies = [
        pltpu.make_async_copy(src, dst, sem.at[number])
        for number, (src, dst) in enumerate(((res, res_out), (grad, grad_out), (curv, curv_out)))
    ]
    for copy in copies:
        copy.start()
    for copy in copies:
        copy.wait()


def body(coherency, observed, flags, tile_map, jones):
    vmem, hbm = (pl.BlockSpec(memory_space=m) for m in (pltpu.VMEM, pltpu.HBM))
    scratch = [
        pltpu.VMEM((2, 6, 12, 8, 256), BF16),
        pltpu.VMEM((2, 12, 8, 256), BF16),
        pltpu.VMEM((2, 6, 192, 128), F32),
        pltpu.VMEM((2, 192, 128), F32),
        pltpu.VMEM((6, 2, 8, 3, 8, 128), F32),
        pltpu.VMEM((2, 2, 2, 6, 8, 128), F32),
        pltpu.VMEM((6, 2, 8, 3, 8, 128), F32),
        pltpu.VMEM((6, 2, 8, 3, 8, 128), F32),
        pltpu.VMEM((8, 2, 3, 8, 128), F32),
        pltpu.VMEM((2, 7, 3, 8, 128), F32),
        pltpu.VMEM((2, 8, 3, 8, 128), F32),
        pltpu.VMEM((2, 3, 8, 128), F32),
        pltpu.VMEM((16, 8, 256), F32),
        pltpu.VMEM((16, 8, 256), F32),
        pltpu.VMEM((TILES, 4, 128), F32),
        pltpu.VMEM((TILES - 1, 4, 128), F32),
        pltpu.VMEM((TILES, 3, 128), F32),
        pltpu.VMEM((2, 256, 256), BF16),
        pltpu.VMEM((2, 256, 256), BF16),
        pltpu.VMEM((48, 256), F32),
        pltpu.SMEM((2, 3), jnp.int32),
        pltpu.SMEM((2, 2), jnp.int32),
        pltpu.VMEM((6, 8, 8), F32),
        pltpu.SemaphoreType.DMA((5,)),
        pltpu.SemaphoreType.DMA((4,)),
        pltpu.SemaphoreType.DMA((6,)),
        pltpu.SemaphoreType.DMA((Z,)),
    ]
    summed = pl.pallas_call(
        kernel,
        out_shape=(
            jax.ShapeDtypeStruct((192, 128), F32),
            jax.ShapeDtypeStruct((4, 128), F32),
        ),
        in_specs=[hbm] * 5,
        out_specs=(vmem, vmem),
        scratch_shapes=scratch,
        compiler_params=pltpu.CompilerParams(
            collective_id=0, has_side_effects=True, vmem_limit_bytes=40 * 1024 * 1024
        ),
    )(*(pltpu.with_memory_space_constraint(x, pltpu.HBM) for x in (coherency, observed, flags, tile_map, jones)))
    shapes = ((2, 12, 8, 32), (6, 8, 8), (6, 2, 8))
    return pl.pallas_call(
        unpack,
        out_shape=tuple(jax.ShapeDtypeStruct(shape, F32) for shape in shapes),
        in_specs=[vmem, vmem],
        out_specs=(hbm, hbm, hbm),
        scratch_shapes=[pltpu.VMEM(shape, F32) for shape in shapes] + [pltpu.SemaphoreType.DMA((3,))],
        compiler_params=pltpu.CompilerParams(vmem_limit_bytes=8 * 1024 * 1024),
    )(*summed)


def solution(mesh):
    return jax.shard_map(
        body,
        mesh=mesh,
        in_specs=(
            P("tile", "dir", None, None, None),
            P("tile", None, None, None),
            P("tile", None),
            P("tile", None),
            P("dir", None, "tile"),
        ),
        out_specs=(P("tile", None, None, "dir"), P("dir", None, "tile"), P("dir", None, "tile")),
        check_vma=False,
    )
```
